256 devices in a mesh: row: 32 (over x_lo, z, core), col: 8 (over x_hi, y).
Axes of the slice: x: 4 (x_hi: 2, x_lo: 2; x = x_hi * 2 + x_lo), y: 4, z: 8, core: 2. Of those that a mesh axis runs over, the one named last changes fastest.
Arguments:
- embed: float32 [1024, 512], P('row', 'col'), may hold values from -6 to 6
- proj: float32 [512, 48], P('col'), may hold values from -0.25 to 0.25
- pair_in: float32 [48, 1024, 1024], P(None, 'row', 'col'), may hold values from -6 to 6
- kernels: float32 [2, 48, 48, 3, 3], replicated, may hold values from -0.3125 to 0.3125
- dilation: int32 [2], replicated, may hold values from 1 to 4, as said below
- cotangent: float32 [48, 1024, 1024], P(None, 'row', 'col'), may hold values from -0.75 to 0.75
Outputs:
- pair_out: float32 [48, 1024, 1024], P(None, 'row', 'col')
- embed_grad: float32 [1024, 512], P('row', 'col')
The draws below stay inside these ranges and needn't reach their ends.
Inputs may be any that keep to these rules, and one draw needn't show every extreme that they name: Each dilation is 1 to 4, and one of them equals 4.
All inputs are finite; a program needn't handle non-finite values.
Results may differ from the reference program's by a relative error of at most 0.00011.
Values sent between devices are 32-bit elements; how exact they have to be, the bound alone decides.
No kernel may reach another device: no remote copies, remote signals or barrier semaphores. Data moves between devices by JAX's collectives and lax.ppermute only.
A program may use at most 64 MiB of HBM per device.

```python
import jax
import jax.numpy as jnp
from jax import lax

D = 512
C = 48
LAYERS = 2
LARGEST_DILATE = 4
BINS = 1024


def draw_dilation(key, part):
    key = jax.random.fold_in(key, 7)
    first_key, second_key = jax.random.split(key)
    values = jax.random.randint(first_key, (LAYERS,), 1, LARGEST_DILATE + 1)
    chosen = jax.random.randint(second_key, (), 0, LAYERS)
    return jnp.where(jnp.arange(LAYERS) == chosen, LARGEST_DILATE, values).astype(jnp.int32)


def shard_levels(own_key, extent, cuts, low, top_value):
    level, own = 1.0, jax.random.fold_in(own_key, 6)
    for position, shards_of in cuts:
        steps = jnp.exp(jax.random.uniform(jax.random.fold_in(own, position), (shards_of,), jnp.float32, low / len(cuts), top_value / len(cuts)))
        level = level * jnp.repeat(steps, extent[position] // shards_of).reshape([-1 if axis == position else 1 for axis in range(len(extent))])
    return level


def bell_draw(own_key, dims, width, bound, cuts=(), dtype=jnp.bfloat16):
    entries = jax.random.normal(own_key, dims, jnp.float32) * width
    if len(cuts) > 0:
        entries = shard_levels(own_key, dims, cuts, -0.22, 0.18) * entries
    return jnp.clip(entries, min=-bound, max=bound).astype(dtype)


def setup_inputs(seed: int = 0) -> dict:
    streams_of = jax.random.split(jax.random.key(seed), 7)
    embed = bell_draw(streams_of[0], (BINS, D), 1.0, 6.0, ((0, 32), (1, 8)), jnp.float32)
    proj = bell_draw(streams_of[1], (D, C), D ** -0.5, 0.25, ((0, 8),), jnp.float32)
    pair_in = bell_draw(streams_of[2], (C, BINS, BINS), 1.0, 6.0, ((1, 32), (2, 8)), jnp.float32)
    kernels = bell_draw(streams_of[3], (LAYERS, C, C, 3, 3), (9 * C) ** -0.5, 0.3125, (), jnp.float32)
    dilation = draw_dilation(jax.random.fold_in(streams_of[6], 71), 0)
    cotangent = bell_draw(streams_of[5], (C, BINS, BINS), (BINS // 16) ** -0.5, 0.75, ((1, 32), (2, 8)), jnp.float32)
    return dict(embed=embed, proj=proj, pair_in=pair_in, kernels=kernels, dilation=dilation, cotangent=cotangent)


def dilated_conv_layer(pair_field, kernel_weight, dilation_step):
    padded_field = jnp.pad(pair_field, ((0, 0), (LARGEST_DILATE, LARGEST_DILATE), (LARGEST_DILATE, LARGEST_DILATE)))
    total = jnp.zeros(pair_field.shape, jnp.float32)
    zero_index = jnp.zeros((), jnp.int32)
    for kernel_tap_row in range(3):
        for kernel_tap_column in range(3):
            first_row = (LARGEST_DILATE + (kernel_tap_row - 1) * dilation_step).astype(jnp.int32)
            first_column = (LARGEST_DILATE + (kernel_tap_column - 1) * dilation_step).astype(jnp.int32)
            shifted = lax.dynamic_slice(padded_field, (zero_index, first_row, first_column), pair_field.shape)
            total = total + jnp.einsum('oc,cij->oij', kernel_weight[:, :, kernel_tap_row, kernel_tap_column], shifted, precision=lax.Precision.HIGHEST)
    return total

def forward(embed, proj, pair_in, kernels, dilation):
    fields = jnp.dot(proj.T, embed.T, precision=lax.Precision.HIGHEST)
    state = pair_in + fields[:, :, None] + fields[:, None, :]
    for layer in range(LAYERS):
        state = state + jnp.tanh(dilated_conv_layer(state, kernels[layer], dilation[layer]))
    return state

def reference(embed, proj, pair_in, kernels, dilation, cotangent):

    def closure(values):
        return forward(values, proj, pair_in, kernels, dilation)
    pair_out, pullback = jax.vjp(closure, embed)
    embed_grad, = pullback(cotangent)
    return (pair_out, embed_grad)
```

```python
import functools

import jax
import jax.numpy as jnp
from jax import lax
from jax.experimental import pallas as pl
from jax.experimental.pallas import tpu as pltpu
from jax.sharding import PartitionSpec as P

C = 48
ROWS = 32
COLS = 128
HALO = 12
GHALO = 4
EXT = ROWS + 2 * HALO
GEXT = ROWS + 2 * GHALO
TAPS = 9 * C
BINS = 1024
PEERS = 16
F32 = jnp.float32
BF16 = jnp.bfloat16
VMEM = pl.BlockSpec(memory_space=pltpu.VMEM)
SMEM = pl.BlockSpec(memory_space=pltpu.SMEM)
PARAMS = pltpu.CompilerParams(vmem_limit_bytes=56 * 2**20)


def lanes_of(rows, width=COLS):
    return lax.broadcasted_iota(jnp.int32, (rows, width), 1)


def turn(value, shift):
    width = value.shape[-1]
    if isinstance(shift, int):
        shift = shift % width
        if shift == 0:
            return value
    return pltpu.roll(value, shift, value.ndim - 1)


def spread(first, second):
    low = lanes_of(C // 2) < 64
    top = jnp.where(low, first, turn(second, 64))
    bottom = jnp.where(low, turn(first, 64), second)
    return jnp.concatenate([top, bottom], axis=0)


def packed(value):
    low = lanes_of(C // 2) < 64
    top, bottom = value[: C // 2], value[C // 2 :]
    first = jnp.where(low, top, turn(bottom, 64))
    second = jnp.where(low, turn(top, 64), bottom)
    return first, second


def project_kernel(scal, embed, proj, out):
    core = scal[2] % 2
    part = lax.dot_general(
        proj[...].T, embed[...].T, (((1,), (0,)), ((), ())),
        precision=lax.Precision.HIGHEST, preferred_element_type=F32,
    )
    part = jnp.concatenate([part, jnp.zeros((C, COLS - ROWS), F32)], axis=1)
    mine = turn(part[: C // 2], 32 * core) + turn(part[C // 2 :], 64 + 32 * core)
    for peer in range(PEERS):
        out[peer] = mine


def strips_kernel(pair, cot, above, below, xm, gm, to_left, to_right):
    for e in range(HALO):
        xm[e] = above[pl.ds(e, C, stride=16), :]
        xm[e + HALO + ROWS] = below[pl.ds(e, C, stride=16), :]
    for e in range(GHALO):
        gm[e] = above[pl.ds(e + HALO, C, stride=16), :]
        gm[e + GHALO + ROWS] = below[pl.ds(e + HALO, C, stride=16), :]
    for i in range(ROWS):
        xm[i + HALO] = pair[pl.ds(i, C, stride=ROWS), :]
        gm[i + GHALO] = cot[pl.ds(i, C, stride=ROWS), :]
    lane = lanes_of(C)

    def body(k, carry):
        g_first = jnp.clip(k - 1, 0, 4) * 8
        left = jnp.zeros((C, COLS), F32)
        right = jnp.zeros((C, COLS), F32)
        for s in range(8):
            x = xm[8 * k + s]
            g = gm[g_first + s]
            slot = (lane >= 16 * s) & (lane < 16 * s + 16)
            to_l = jnp.where(lane < 12, x, turn(g, 12))
            to_r = jnp.where(lane < 116, turn(g, -12), x)
            left = jnp.where(slot, turn(to_l, 16 * s), left)
            right = jnp.where(slot, turn(to_r, 16 * s - 112), right)
        to_left[k] = left
        to_right[k] = right
        return carry

    lax.fori_loop(0, EXT // 8, body, 0)


def dot(a, b):
    return jnp.dot(a, b, preferred_element_type=F32)


def split(value):
    hi = value.astype(BF16)
    lo = (value - hi.astype(F32)).astype(BF16)
    return hi, lo


def weighted(weights, x_hi, x_lo):
    both = dot(weights, x_hi)
    low = dot(weights[:C], x_lo)
    return both[:C] + (both[C:] + low)


def main_kernel(
    scal, xm, gm, from_left, from_right, fields, mats, pair_out, send,
    x0, xh, xl, yh, yl, sh, sl, gb, t0s, s0s, g1s, wts, buf,
):
    d0, d1, row, col = scal[0], scal[1], scal[2], scal[3]
    lane = lanes_of(C)
    for m in range(4):
        hi, lo = split(mats[m])
        wts[m, :C] = hi
        wts[m, C:] = lo
    own_u = spread(fields[2 * col], fields[2 * col + 1])
    side_u = spread(fields[jnp.minimum(2 * col + 2, PEERS - 1)], fields[jnp.maximum(2 * col - 1, 0)])
    group, core = row // 2, row % 2
    near = jnp.clip(group - 1 + core, 0, PEERS - 1)
    far = jnp.clip(group + core, 0, PEERS - 1)
    row_u = turn(spread(fields[near], fields[far]), 76 + 32 * core)
    inside = ((lane < HALO) & (col < 7)) | ((lane >= COLS - HALO) & (col > 0))
    side_mask = jnp.where(inside, 1.0, 0.0).astype(F32)
    full_mask = jnp.concatenate([jnp.ones((C, COLS), F32), side_mask], axis=1)
    side_u = side_u * side_mask

    def row_mask(e):
        at = row * ROWS + e - HALO
        return jnp.where((at >= 0) & (at < BINS), 1.0, 0.0).astype(F32)

    def put_shifted(hi_ref, lo_ref, e, value, step, width):
        n = value.shape[-1]
        for b, shift in enumerate((n - step, 0, step)):
            moved = value if b == 1 else turn(value, shift)
            hi, lo = split(moved[:, :width])
            hi_ref[e, b * C : (b + 1) * C] = hi
            lo_ref[e, b * C : (b + 1) * C] = lo

    def assemble(k, carry):
        ur = turn(row_u, (COLS - 8 * k) % COLS)
        fl = from_left[k]
        fr = from_right[k]
        for s in range(8):
            e = 8 * k + s
            keep = row_mask(e)
            ui = jnp.broadcast_to(ur[:, s : s + 1], (C, COLS)) * keep
            main = xm[e] + (ui + own_u * keep)
            side = jnp.where(
                lane < HALO, turn(fr, -16 * s),
                jnp.where(lane >= COLS - HALO, turn(fl, 112 - 16 * s), 0.0),
            )
            side = side + (ui * side_mask + side_u * keep)
            whole = jnp.concatenate([main, side], axis=1)
            x0[e] = whole
            put_shifted(xh, xl, e, whole, -d0 % 256, 2 * COLS)
        return carry

    lax.fori_loop(0, EXT // 8, assemble, 0)

    def assemble_g(k, carry):
        fl = from_left[k + 1]
        fr = from_right[k + 1]
        for s in range(8):
            gb[8 * k + s] = jnp.where(
                lane < GHALO, turn(fr, -(16 * s + 12)),
                jnp.where(lane >= COLS - GHALO, turn(fl, 124 - 16 * s), 0.0),
            )
        return carry

    lax.fori_loop(0, GEXT // 8, assemble_g, 0)

    def stacked(ref, lowest, middle, highest):
        return jnp.concatenate([ref[lowest], ref[middle], ref[highest]], axis=0)

    def first(i, carry):
        e = i + 4
        acc = weighted(
            wts[0], stacked(xh, e - d0, e, e + d0), stacked(xl, e - d0, e, e + d0)
        )
        t = jnp.tanh(acc)
        t0s[e] = t[:, :COLS]
        h = x0[e] + t * (full_mask * row_mask(e))
        x0[e] = h
        put_shifted(yh, yl, e, h, -d1 % 256, 2 * COLS)
        return carry

    lax.fori_loop(0, EXT - 8, first, 0, unroll=4)

    def second(e, own):
        acc = weighted(
            wts[1], stacked(yh, e - d1, e, e + d1), stacked(yl, e - d1, e, e + d1)
        )
        t = jnp.tanh(acc)
        if own:
            pair_out[pl.ds(e - HALO, C, stride=ROWS), :] = x0[e, :, :COLS] + t[:, :COLS]
        g = jnp.concatenate([gm[e - 8], gb[e - 8]], axis=1)
        scaled = g * (1.0 - t * t)
        put_shifted(sh, sl, e - 8, scaled, d1, COLS)

    def second_own(i, carry):
        second(i + HALO, True)
        return carry

    for e in (8, 9, 10, 11, 44, 45, 46, 47):
        second(e, False)
    lax.fori_loop(0, ROWS, second_own, 0, unroll=4)

    def third(i, carry):
        parts_hi, parts_lo = [], []
        for k in range(2):
            q = 2 * i + k + GHALO
            parts_hi.append(stacked(sh, q + d1, q, q - d1))
            parts_lo.append(stacked(sl, q + d1, q, q - d1))
        acc = weighted(
            wts[2], jnp.concatenate(parts_hi, axis=1), jnp.concatenate(parts_lo, axis=1)
        )
        for k in range(2):
            at = 2 * i + k
            g1 = gm[at + GHALO] + acc[:, k * COLS : (k + 1) * COLS]
            t = t0s[at + HALO]
            g1s[at] = g1
            s0s[at] = g1 * (1.0 - t * t)
        return carry

    lax.fori_loop(0, ROWS // 2, third, 0, unroll=4)

    at_col = col * COLS + lane
    keep_up = jnp.where(at_col < BINS - d0, 1.0, 0.0).astype(F32)
    keep_down = jnp.where(at_col >= d0, 1.0, 0.0).astype(F32)
    zero = jnp.zeros((C, COLS), F32)

    def sums(i, carry):
        s0, g1 = s0s[i], g1s[i]
        at = row * ROWS + i
        up = jnp.where(at < BINS - d0, 1.0, 0.0).astype(F32)
        down = jnp.where(at >= d0, 1.0, 0.0).astype(F32)
        cg, cd, c0, cu, rg, rd, r0, ru = carry
        here = lane == i

        def place(total, value):
            return jnp.where(here, jnp.sum(value, axis=1, keepdims=True), total)

        return (
            cg + g1, cd + s0 * down, c0 + s0, cu + s0 * up,
            place(rg, g1), place(rd, s0 * keep_down), place(r0, s0), place(ru, s0 * keep_up),
        )

    cg, cd, c0, cu, rg, rd, r0, ru = lax.fori_loop(0, ROWS, sums, (zero,) * 8)
    blocks = []
    for part in (cd, c0, cu):
        wide = jnp.concatenate([part, zero], axis=1)
        blocks += [turn(wide, 256 - d0), wide, turn(wide, d0)]
    col_x = jnp.concatenate(blocks, axis=0)
    blocks = []
    for a in range(3):
        for part in (rd, r0, ru):
            blocks.append((turn(part, COLS - d0), part, turn(part, d0))[a])
    row_x = jnp.concatenate(blocks, axis=0)
    hi, lo = split(jnp.concatenate([col_x, row_x], axis=1))
    made = weighted(wts[3], hi, lo)
    buf[...] = jnp.zeros(buf.shape, F32)

    def add(first_at, second_at, value):
        one, two = packed(value)
        buf[first_at] = buf[first_at] + one
        buf[second_at] = buf[second_at] + two

    add(2 * col + 1, 2 * col + 2, cg + made[:, :COLS])
    add(2 * col + 3, 2 * col, made[:, COLS : 2 * COLS])
    add(group + core, group + core + 1, turn(rg + made[:, 2 * COLS :], 64 - 32 * core))
    send[...] = buf[1 : PEERS + 1]


def finish_kernel(scal, parts, proj, out):
    core = scal[2] % 2
    total = parts[0]
    for peer in range(1, PEERS):
        total = total + parts[peer]
    both = jnp.concatenate([turn(total, 128 - 32 * core), turn(total, 64 - 32 * core)], axis=0)
    grad = lax.dot_general(
        proj[...], both, (((1,), (0,)), ((), ())),
        precision=lax.Precision.HIGHEST, preferred_element_type=F32,
    )
    out[...] = grad.T[:ROWS]


def local(embed, proj, pair_in, kernels, dilation, cotangent):
    rows, cols = 32, 8
    row = lax.axis_index("row")
    col = lax.axis_index("col")
    scal = jnp.stack([dilation[0], dilation[1], row, col]).astype(jnp.int32)
    down = [(i, i + 1) for i in range(rows - 1)]
    up = [(i + 1, i) for i in range(rows - 1)]
    right = [(i, i + 1) for i in range(cols - 1)]
    left = [(i + 1, i) for i in range(cols - 1)]
    same_core = [[2 * i + core for i in range(PEERS)] for core in range(2)]
    chips = [[(2 * g + core) * cols + c for core in range(2) for c in range(cols)] for g in range(PEERS)]

    low_edge = jnp.concatenate([pair_in[:, ROWS - HALO :], cotangent[:, ROWS - GHALO :]], axis=1)
    high_edge = jnp.concatenate([pair_in[:, :HALO], cotangent[:, :GHALO]], axis=1)
    above = lax.ppermute(low_edge, "row", down)
    below = lax.ppermute(high_edge, "row", up)

    packs = jax.ShapeDtypeStruct((PEERS, C // 2, COLS), F32)
    parts = pl.pallas_call(
        project_kernel, in_specs=[SMEM, VMEM, VMEM], out_specs=VMEM, out_shape=packs, name="project",
    )(scal, embed, proj)
    parts = lax.all_to_all(parts, ("row", "col"), 0, 0, tiled=True, axis_index_groups=chips)

    xm, gm, to_left, to_right = pl.pallas_call(
        strips_kernel,
        in_specs=[VMEM] * 4,
        out_specs=[VMEM] * 4,
        out_shape=[
            jax.ShapeDtypeStruct((EXT, C, COLS), F32),
            jax.ShapeDtypeStruct((GEXT, C, COLS), F32),
            jax.ShapeDtypeStruct((EXT // 8, C, COLS), F32),
            jax.ShapeDtypeStruct((EXT // 8, C, COLS), F32),
        ],
        compiler_params=PARAMS,
        name="strips",
    )(
        pair_in.reshape(C * ROWS, COLS), cotangent.reshape(C * ROWS, COLS),
        above.reshape(C * 16, COLS), below.reshape(C * 16, COLS),
    )
    from_left = lax.ppermute(to_right, "col", right)
    from_right = lax.ppermute(to_left, "col", left)

    own = jnp.sum(parts, axis=0)
    fields = lax.all_to_all(
        jnp.broadcast_to(own, (PEERS,) + own.shape), "row", 0, 0, tiled=True, axis_index_groups=same_core
    )

    forward = kernels.transpose(0, 1, 3, 4, 2).reshape(2, C, TAPS)
    backward = kernels.transpose(0, 2, 3, 4, 1).reshape(2, C, TAPS)
    mats = jnp.stack([forward[0], forward[1], backward[1], backward[0]])
    pair_out, send = pl.pallas_call(
        main_kernel,
        in_specs=[SMEM] + [VMEM] * 6,
        out_specs=[VMEM] * 2,
        out_shape=[jax.ShapeDtypeStruct((C * ROWS, COLS), F32), packs],
        scratch_shapes=[
            pltpu.VMEM((EXT, C, 2 * COLS), F32),
            pltpu.VMEM((EXT, 3 * C, 2 * COLS), BF16),
            pltpu.VMEM((EXT, 3 * C, 2 * COLS), BF16),
            pltpu.VMEM((EXT, 3 * C, 2 * COLS), BF16),
            pltpu.VMEM((EXT, 3 * C, 2 * COLS), BF16),
            pltpu.VMEM((GEXT, 3 * C, COLS), BF16),
            pltpu.VMEM((GEXT, 3 * C, COLS), BF16),
            pltpu.VMEM((GEXT, C, COLS), F32),
            pltpu.VMEM((EXT, C, COLS), F32),
            pltpu.VMEM((ROWS, C, COLS), F32),
            pltpu.VMEM((ROWS, C, COLS), F32),
            pltpu.VMEM((4, 2 * C, TAPS), BF16),
            pltpu.VMEM((PEERS + 2, C // 2, COLS), F32),
        ],
        compiler_params=PARAMS,
        name="layers",
    )(scal, xm, gm, from_left, from_right, fields, mats)

    got = lax.all_to_all(send, "row", 0, 0, tiled=True, axis_index_groups=same_core)
    own = jnp.sum(got, axis=0)
    got = lax.all_to_all(
        jnp.broadcast_to(own, (PEERS,) + own.shape), ("row", "col"), 0, 0, tiled=True, axis_index_groups=chips
    )
    embed_grad = pl.pallas_call(
        finish_kernel, in_specs=[SMEM, VMEM, VMEM], out_specs=VMEM,
        out_shape=jax.ShapeDtypeStruct((ROWS, 64), F32), name="finish",
    )(scal, got, proj)
    return (pair_out.reshape(C, ROWS, COLS), embed_grad)


def solution(mesh):
    in_specs = (
        P("row", "col"),
        P("col", None),
        P(None, "row", "col"),
        P(),
        P(),
        P(None, "row", "col"),
    )
    out_specs = (P(None, "row", "col"), P("row", "col"))
    return jax.shard_map(local, mesh=mesh, in_specs=in_specs, out_specs=out_specs, check_vma=False)
```

```python
import functools

import jax
import jax.numpy as jnp
from jax import lax
from jax.experimental import pallas as pl
from jax.experimental.pallas import tpu as pltpu
from jax.sharding import PartitionSpec as P

C = 48
ROWS = 32
COLS = 128
HALO = 12
GHALO = 4
EXT = ROWS + 2 * HALO
GEXT = ROWS + 2 * GHALO
TAPS = 9 * C
BINS = 1024
PEERS = 16
F32 = jnp.float32
BF16 = jnp.bfloat16
VMEM = pl.BlockSpec(memory_space=pltpu.VMEM)
SMEM = pl.BlockSpec(memory_space=pltpu.SMEM)


def lanes_of(rows, width=COLS):
    return lax.broadcasted_iota(jnp.int32, (rows, width), 1)


def turn(value, shift):
    width = value.shape[-1]
    if isinstance(shift, int):
        shift = shift % width
        if shift == 0:
            return value
    return pltpu.roll(value, shift, value.ndim - 1)


def spread(first, second):
    low = lanes_of(C // 2) < 64
    top = jnp.where(low, first, turn(second, 64))
    bottom = jnp.where(low, turn(first, 64), second)
    return jnp.concatenate([top, bottom], axis=0)


def packed(value):
    low = lanes_of(C // 2) < 64
    top, bottom = value[: C // 2], value[C // 2 :]
    first = jnp.where(low, top, turn(bottom, 64))
    second = jnp.where(low, turn(top, 64), bottom)
    return first, second


def project_kernel(embed, proj_t, out):
    core = lax.axis_index("row") % 2
    part = lax.dot_general(
        proj_t[...], embed[...], (((1,), (1,)), ((), ())),
        precision=lax.Precision.HIGHEST, preferred_element_type=F32,
    )
    part = jnp.concatenate([part, jnp.zeros((C, COLS - ROWS), F32)], axis=1)
    mine = turn(part[: C // 2], 32 * core) + turn(part[C // 2 :], 64 + 32 * core)
    for peer in range(PEERS):
        out[peer] = mine


def source(e):
    if e < HALO:
        return 0, e
    if e < HALO + ROWS:
        return 1, e - HALO
    return 2, e - HALO - ROWS


def edges_kernel(pair, cot, low, high):
    for e in range(HALO):
        low[e] = pair[pl.ds(e + ROWS - HALO, C, stride=ROWS), :]
        high[e] = pair[pl.ds(e, C, stride=ROWS), :]
    for e in range(GHALO):
        low[e + HALO] = cot[pl.ds(e + ROWS - GHALO, C, stride=ROWS), :]
        high[e + HALO] = cot[pl.ds(e, C, stride=ROWS), :]


def combine_kernel(parts, out):
    total = parts[0]
    for peer in range(1, PEERS):
        total = total + parts[peer]
    for peer in range(PEERS):
        out[peer] = total


def strips_kernel(pair, cot, above, below, to_left, to_right):
    lane = lanes_of(C)
    for k in range(EXT // 8):
        left = jnp.zeros((C, COLS), F32)
        right = jnp.zeros((C, COLS), F32)
        for s in range(8):
            e = 8 * k + s
            where_, at = source(e)
            if where_ == 1:
                x = pair[pl.ds(at, C, stride=ROWS), :]
                g = cot[pl.ds(at, C, stride=ROWS), :]
            else:
                ref = (above, None, below)[where_]
                x = ref[at]
                g = None
                if 8 <= e < HALO:
                    g = above[HALO + e - 8]
                if HALO + ROWS <= e < HALO + ROWS + GHALO:
                    g = below[HALO + at]
            to_l, to_r = x, x
            if g is not None:
                to_l = jnp.where(lane < 12, x, turn(g, 12))
                to_r = jnp.where(lane < 116, turn(g, -12), x)
            slot = (lane >= 16 * s) & (lane < 16 * s + 16)
            left = jnp.where(slot, turn(to_l, 16 * s), left)
            right = jnp.where(slot, turn(to_r, 16 * s - 112), right)
        to_left[k] = left
        to_right[k] = right


def weights_kernel(taps, out):
    for m, (layer, flip) in enumerate(((0, False), (1, False), (1, True), (0, True))):
        tiles = [taps[9 * layer + n] for n in range(9)]
        if flip:
            tiles = [tile.T for tile in tiles]
        hi, lo = split(jnp.concatenate(tiles, axis=1))
        out[m, :C] = hi
        out[m, C:] = lo


def dot(a, b):
    return jnp.dot(a, b, preferred_element_type=F32)


def split(value):
    hi = value.astype(BF16)
    lo = (value - hi.astype(F32)).astype(BF16)
    return hi, lo


def weighted(weights, x_hi, x_lo):
    both = dot(weights, x_hi)
    low = dot(weights[:C], x_lo)
    return both[:C] + (both[C:] + low)


def main_kernel(
    dil, pair, cot, above, below, from_left, from_right, fields, wts, pair_out, send,
    x0, xh, xl, yh, yl, sh, sl, gm, gb, t0s, s0s, g1s, buf,
):
    d0, d1 = dil[0], dil[1]
    row, col = lax.axis_index("row"), lax.axis_index("col")
    lane = lanes_of(C)
    own_u = spread(fields[2 * col], fields[2 * col + 1])
    side_u = spread(fields[jnp.minimum(2 * col + 2, PEERS - 1)], fields[jnp.maximum(2 * col - 1, 0)])
    group, core = row // 2, row % 2
    near = jnp.clip(group - 1 + core, 0, PEERS - 1)
    far = jnp.clip(group + core, 0, PEERS - 1)
    row_u = turn(spread(fields[near], fields[far]), 76 + 32 * core)
    inside = ((lane < HALO) & (col < 7)) | ((lane >= COLS - HALO) & (col > 0))
    side_mask = jnp.where(inside, 1.0, 0.0).astype(F32)
    side_u = side_u * side_mask

    def row_mask(e):
        at = row * ROWS + e - HALO
        return jnp.where((at >= 0) & (at < BINS), 1.0, 0.0).astype(F32)

    def put_shifted(hi_ref, lo_ref, e, main, side, step, swap):
        low = lane < step
        high = lane >= COLS - step
        for ref, a, b in zip((hi_ref, lo_ref), split(main), split(side)):
            a_up, b_up = turn(a, step), turn(b, step)
            a_down, b_down = turn(a, COLS - step), turn(b, COLS - step)
            up = jnp.where(low, b_up, a_up)
            down = jnp.where(high, b_down, a_down)
            if swap:
                ref[e, :C] = down
                ref[e, C : 2 * C] = a
                ref[e, 2 * C :] = up
            else:
                ref[e, :C, :COLS] = up
                ref[e, :C, COLS:] = jnp.where(low, a_up, b_up)
                ref[e, C : 2 * C, :COLS] = a
                ref[e, C : 2 * C, COLS:] = b
                ref[e, 2 * C :, :COLS] = down
                ref[e, 2 * C :, COLS:] = jnp.where(high, a_down, b_down)

    def assemble(e, k, s, x, ur):
        fl, fr = from_left[k], from_right[k]
        keep = row_mask(e)
        ui = jnp.broadcast_to(ur, (C, COLS)) * keep
        main = x + (ui + own_u * keep)
        side = jnp.where(
            lane < HALO, turn(fr, -16 * s),
            jnp.where(lane >= COLS - HALO, turn(fl, 112 - 16 * s), 0.0),
        )
        side = side + (ui * side_mask + side_u * keep)
        x0[e, :, :COLS] = main
        x0[e, :, COLS:] = side
        put_shifted(xh, xl, e, main, side, d0, False)

    def assemble_g(f, k, s, g):
        gm[f] = g
        gb[f] = jnp.where(
            lane < GHALO, turn(from_right[k], -(16 * s + 12)),
            jnp.where(lane >= COLS - GHALO, turn(from_left[k], 124 - 16 * s), 0.0),
        )

    for e in tuple(range(HALO)) + tuple(range(HALO + ROWS, EXT)):
        where_, at = source(e)
        ref = above if where_ == 0 else below
        assemble(e, e // 8, e % 8, ref[at], row_u[:, e : e + 1])
        if 8 <= e < HALO:
            assemble_g(e - 8, e // 8, e % 8, above[HALO + e - 8])
        if HALO + ROWS <= e < HALO + ROWS + GHALO:
            assemble_g(e - 8, e // 8, e % 8, below[HALO + at])

    def assemble_own(q, carry):
        ur = turn(row_u, (COLS - HALO - 8 * q) % COLS)
        for s in range(8):
            k, slot = q + 1 + (s + 4) // 8, (s + 4) % 8
            at = 8 * q + s
            assemble(at + HALO, k, slot, pair[pl.ds(at, C, stride=ROWS), :], ur[:, s : s + 1])
            assemble_g(at + GHALO, k, slot, cot[pl.ds(at, C, stride=ROWS), :])
        return carry

    lax.fori_loop(0, ROWS // 8, assemble_own, 0)

    def stacked(ref, lowest, middle, highest):
        return jnp.concatenate([ref[lowest], ref[middle], ref[highest]], axis=0)

    def first(i, carry):
        e = i + 4
        acc = weighted(
            wts[0], stacked(xh, e - d0, e, e + d0), stacked(xl, e - d0, e, e + d0)
        )
        t = jnp.tanh(acc)
        t0s[e] = t[:, :COLS]
        keep = row_mask(e)
        main = x0[e, :, :COLS] + t[:, :COLS] * keep
        side = x0[e, :, COLS:] + t[:, COLS:] * (side_mask * keep)
        x0[e, :, :COLS] = main
        put_shifted(yh, yl, e, main, side, d1, False)
        return carry

    lax.fori_loop(0, EXT - 8, first, 0, unroll=16)

    def second(e, own):
        acc = weighted(
            wts[1], stacked(yh, e - d1, e, e + d1), stacked(yl, e - d1, e, e + d1)
        )
        t = jnp.tanh(acc)
        if own:
            pair_out[pl.ds(e - HALO, C, stride=ROWS), :] = x0[e, :, :COLS] + t[:, :COLS]
        slope = 1.0 - t * t
        put_shifted(sh, sl, e - 8, gm[e - 8] * slope[:, :COLS], gb[e - 8] * slope[:, COLS:], d1, True)

    def second_own(i, carry):
        second(i + HALO, True)
        return carry

    for e in (8, 9, 10, 11, 44, 45, 46, 47):
        second(e, False)
    lax.fori_loop(0, ROWS, second_own, 0, unroll=16)

    def third(i, carry):
        parts_hi, parts_lo = [], []
        for k in range(2):
            q = 2 * i + k + GHALO
            parts_hi.append(stacked(sh, q + d1, q, q - d1))
            parts_lo.append(stacked(sl, q + d1, q, q - d1))
        acc = weighted(
            wts[2], jnp.concatenate(parts_hi, axis=1), jnp.concatenate(parts_lo, axis=1)
        )
        for k in range(2):
            at = 2 * i + k
            g1 = gm[at + GHALO] + acc[:, k * COLS : (k + 1) * COLS]
            t = t0s[at + HALO]
            g1s[at] = g1
            s0s[at] = g1 * (1.0 - t * t)
        return carry

    lax.fori_loop(0, ROWS // 2, third, 0, unroll=8)

    lane8 = lanes_of(8)
    edge = ((lane8 < d0) & (col == 0)) | ((lane8 >= COLS - d0) & (col == 7))
    edge_lanes = jnp.where(edge, 1.0, 0.0).astype(F32)
    first_col = jnp.where(col == 0, 1.0, 0.0).astype(F32)
    last_col = jnp.where(col == 7, 1.0, 0.0).astype(F32)
    pieces = []
    for octet in range(C // 8):
        at = slice(8 * octet, 8 * octet + 8)
        cg = c0 = rg = r0 = re = top = bottom = jnp.zeros((8, COLS), F32)
        for i in range(ROWS):
            s0, g1 = s0s[i, at], g1s[i, at]
            cg, c0 = cg + g1, c0 + s0
            here = lane8 == i
            rg = jnp.where(here, jnp.sum(g1, axis=1, keepdims=True), rg)
            r0 = jnp.where(here, jnp.sum(s0, axis=1, keepdims=True), r0)
            re = jnp.where(here, jnp.sum(s0 * edge_lanes, axis=1, keepdims=True), re)
            if i < GHALO:
                top = top + s0 * jnp.where((row == 0) & (i < d0), 1.0, 0.0).astype(F32)
            if i >= ROWS - GHALO:
                bottom = bottom + s0 * jnp.where((row == 31) & (i >= ROWS - d0), 1.0, 0.0).astype(F32)
        pieces.append((cg, c0 - top, c0, c0 - bottom, rg, r0 - re * first_col, r0, r0 - re * last_col))
    cg, cd, c0, cu, rg, rd, r0, ru = [jnp.concatenate(p, axis=0) for p in zip(*pieces)]
    zero = jnp.zeros((C, COLS), F32)
    blocks = []
    for part in (cd, c0, cu):
        wide = jnp.concatenate([part, zero], axis=1)
        blocks += [turn(wide, 256 - d0), wide, turn(wide, d0)]
    col_x = jnp.concatenate(blocks, axis=0)
    blocks = []
    for a in range(3):
        for part in (rd, r0, ru):
            blocks.append((turn(part, COLS - d0), part, turn(part, d0))[a])
    row_x = jnp.concatenate(blocks, axis=0)
    hi, lo = split(jnp.concatenate([col_x, row_x], axis=1))
    made = weighted(wts[3], hi, lo)
    buf[...] = jnp.zeros(buf.shape, F32)

    def add(first_at, second_at, value):
        one, two = packed(value)
        buf[first_at] = buf[first_at] + one
        buf[second_at] = buf[second_at] + two

    add(2 * col + 1, 2 * col + 2, cg + made[:, :COLS])
    add(2 * col + 3, 2 * col, made[:, COLS : 2 * COLS])
    add(group + core, group + core + 1, turn(rg + made[:, 2 * COLS :], 64 - 32 * core))
    send[...] = buf[1 : PEERS + 1]


def layers(dilation, pair, cot, above, below, from_left, from_right, fields, wts):
    return pl.pallas_call(
        main_kernel,
        in_specs=[SMEM] + [VMEM] * 8,
        out_specs=[VMEM] * 2,
        out_shape=[
            jax.ShapeDtypeStruct((C * ROWS, COLS), F32),
            jax.ShapeDtypeStruct((PEERS, C // 2, COLS), F32),
        ],
        scratch_shapes=[
            pltpu.VMEM((EXT, C, 2 * COLS), F32),
            pltpu.VMEM((EXT, 3 * C, 2 * COLS), BF16),
            pltpu.VMEM((EXT, 3 * C, 2 * COLS), BF16),
            pltpu.VMEM((EXT, 3 * C, 2 * COLS), BF16),
            pltpu.VMEM((EXT, 3 * C, 2 * COLS), BF16),
            pltpu.VMEM((GEXT, 3 * C, COLS), BF16),
            pltpu.VMEM((GEXT, 3 * C, COLS), BF16),
            pltpu.VMEM((GEXT, C, COLS), F32),
            pltpu.VMEM((GEXT, C, COLS), F32),
            pltpu.VMEM((EXT, C, COLS), F32),
            pltpu.VMEM((ROWS, C, COLS), F32),
            pltpu.VMEM((ROWS, C, COLS), F32),
            pltpu.VMEM((PEERS + 2, C // 2, COLS), F32),
        ],
        compiler_params=pltpu.CompilerParams(vmem_limit_bytes=40 * 2**20),
        name="layers",
    )(dilation, pair, cot, above, below, from_left, from_right, fields, wts)


def finish_kernel(parts, proj_t, out):
    core = lax.axis_index("row") % 2
    total = parts[0]
    for peer in range(1, PEERS):
        total = total + parts[peer]
    both = jnp.concatenate([turn(total, 128 - 32 * core), turn(total, 64 - 32 * core)], axis=0)
    grad = lax.dot_general(
        both, proj_t[...], (((0,), (0,)), ((), ())),
        precision=lax.Precision.HIGHEST, preferred_element_type=F32,
    )
    out[...] = grad[:ROWS]


def local(embed, proj, pair_in, kernels, dilation, cotangent):
    rows, cols = 32, 8
    down = [(i, i + 1) for i in range(rows - 1)]
    up = [(i + 1, i) for i in range(rows - 1)]
    right = [(i, i + 1) for i in range(cols - 1)]
    left = [(i + 1, i) for i in range(cols - 1)]
    same_core = [[2 * i + core for i in range(PEERS)] for core in range(2)]
    chips = [[(2 * g + core) * cols + c for core in range(2) for c in range(cols)] for g in range(PEERS)]
    packs = jax.ShapeDtypeStruct((PEERS, C // 2, COLS), F32)
    proj_t = proj.T

    pair = pair_in.reshape(C * ROWS, COLS)
    cot = cotangent.reshape(C * ROWS, COLS)
    low_edge, high_edge = pl.pallas_call(
        edges_kernel, in_specs=[VMEM] * 2, out_specs=[VMEM] * 2,
        out_shape=[jax.ShapeDtypeStruct((HALO + GHALO, C, COLS), F32)] * 2, name="edges",
        compiler_params=pltpu.CompilerParams(vmem_limit_bytes=8 * 2**20),
    )(pair, cot)
    low_edge, high_edge, embed = lax.optimization_barrier((low_edge, high_edge, embed))
    above = lax.ppermute(low_edge, "row", down)
    below = lax.ppermute(high_edge, "row", up)

    parts = pl.pallas_call(
        project_kernel, in_specs=[VMEM, VMEM], out_specs=VMEM, out_shape=packs, name="project",
    )(embed, proj_t)
    parts = lax.all_to_all(parts, ("row", "col"), 0, 0, tiled=True, axis_index_groups=chips)

    to_left, to_right = pl.pallas_call(
        strips_kernel,
        in_specs=[VMEM] * 4,
        out_specs=[VMEM] * 2,
        out_shape=[jax.ShapeDtypeStruct((EXT // 8, C, COLS), F32)] * 2,
        compiler_params=pltpu.CompilerParams(vmem_limit_bytes=8 * 2**20),
        name="strips",
    )(pair, cot, above, below)
    parts, to_left, to_right = lax.optimization_barrier((parts, to_left, to_right))
    from_left = lax.ppermute(to_right, "col", right)
    from_right = lax.ppermute(to_left, "col", left)

    fields = pl.pallas_call(
        combine_kernel, in_specs=[VMEM], out_specs=VMEM, out_shape=packs, name="combine",
        cost_estimate=pl.CostEstimate(flops=0, transcendentals=0, bytes_accessed=64 * 2**20),
    )(parts)
    fields = lax.all_to_all(fields, "row", 0, 0, tiled=True, axis_index_groups=same_core)

    taps = kernels.transpose(0, 3, 4, 1, 2).reshape(18, C, C)
    wts = pl.pallas_call(
        weights_kernel, in_specs=[VMEM], out_specs=VMEM,
        out_shape=jax.ShapeDtypeStruct((4, 2 * C, TAPS), BF16), name="weights",
    )(taps)
    pair_out, send = layers(dilation, pair, cot, above, below, from_left, from_right, fields, wts)

    got = lax.all_to_all(send, "row", 0, 0, tiled=True, axis_index_groups=same_core)
    own = jnp.sum(got, axis=0)
    got = lax.all_to_all(
        jnp.broadcast_to(own, (PEERS,) + own.shape), ("row", "col"), 0, 0, tiled=True, axis_index_groups=chips
    )
    embed_grad = pl.pallas_call(
        finish_kernel, in_specs=[VMEM, VMEM], out_specs=VMEM,
        out_shape=jax.ShapeDtypeStruct((ROWS, 64), F32), name="finish",
    )(got, proj_t)
    return (pair_out.reshape(C, ROWS, COLS), embed_grad)


def solution(mesh):
    in_specs = (
        P("row", "col"),
        P("col", None),
        P(None, "row", "col"),
        P(),
        P(),
        P(None, "row", "col"),
    )
    out_specs = (P(None, "row", "col"), P("row", "col"))
    return jax.shard_map(local, mesh=mesh, in_specs=in_specs, out_specs=out_specs, check_vma=False)
```

```python
import functools

import jax
import jax.numpy as jnp
from jax import lax
from jax.experimental import pallas as pl
from jax.experimental.pallas import tpu as pltpu
from jax.sharding import PartitionSpec as P

C = 48
ROWS = 32
COLS = 128
HALO = 12
GHALO = 4
EXT = ROWS + 2 * HALO
GEXT = ROWS + 2 * GHALO
TAPS = 9 * C
BINS = 1024
PEERS = 16
F32 = jnp.float32
BF16 = jnp.bfloat16
VMEM = pl.BlockSpec(memory_space=pltpu.VMEM)
SMEM = pl.BlockSpec(memory_space=pltpu.SMEM)


def lanes_of(rows, width=COLS):
    return lax.broadcasted_iota(jnp.int32, (rows, width), 1)


def turn(value, shift):
    width = value.shape[-1]
    if isinstance(shift, int):
        shift = shift % width
        if shift == 0:
            return value
    return pltpu.roll(value, shift, value.ndim - 1)


def spread(first, second):
    low = lanes_of(C // 2) < 64
    top = jnp.where(low, first, turn(second, 64))
    bottom = jnp.where(low, turn(first, 64), second)
    return jnp.concatenate([top, bottom], axis=0)


def packed(value):
    low = lanes_of(C // 2) < 64
    top, bottom = value[: C // 2], value[C // 2 :]
    first = jnp.where(low, top, turn(bottom, 64))
    second = jnp.where(low, turn(top, 64), bottom)
    return first, second


def project_kernel(embed, proj_t, out):
    core = lax.axis_index("row") % 2
    part = lax.dot_general(
        proj_t[...], embed[...], (((1,), (1,)), ((), ())),
        precision=lax.Precision.HIGHEST, preferred_element_type=F32,
    )
    part = jnp.concatenate([part, jnp.zeros((C, COLS - ROWS), F32)], axis=1)
    mine = turn(part[: C // 2], 32 * core) + turn(part[C // 2 :], 64 + 32 * core)
    for peer in range(PEERS):
        out[peer] = mine


def partners(mine_is_even, got_a, got_b, at):
    one, two = got_a[at], got_b[at]
    return jnp.where(mine_is_even, two, one), jnp.where(mine_is_even, one, two)


def source(e):
    if e < HALO:
        return 0, e
    if e < HALO + ROWS:
        return 1, e - HALO
    return 2, e - HALO - ROWS


def edges_kernel(pair, cot, to_a, to_b):
    even = lax.axis_index("row") % 2 == 0
    for ref, count, start in ((pair, HALO, 0), (cot, GHALO, HALO)):
        for e in range(count):
            low = ref[pl.ds(e + ROWS - count, C, stride=ROWS), :]
            high = ref[pl.ds(e, C, stride=ROWS), :]
            to_a[start + e] = jnp.where(even, low, high)
            to_b[start + e] = jnp.where(even, high, low)


def strips_kernel(pair, cot, got_a, got_b, to_a, to_b):
    lane = lanes_of(C)
    row_even = lax.axis_index("row") % 2 == 0
    col_even = lax.axis_index("col") % 2 == 0
    for k in range(EXT // 8):
        left = jnp.zeros((C, COLS), F32)
        right = jnp.zeros((C, COLS), F32)
        for s in range(8):
            e = 8 * k + s
            place, at = source(e)
            g = None
            if place == 1:
                x = pair[pl.ds(at, C, stride=ROWS), :]
                g = cot[pl.ds(at, C, stride=ROWS), :]
            elif place == 0:
                x = partners(row_even, got_a, got_b, at)[0]
                if e >= 8:
                    g = partners(row_even, got_a, got_b, HALO + e - 8)[0]
            else:
                x = partners(row_even, got_a, got_b, at)[1]
                if at < GHALO:
                    g = partners(row_even, got_a, got_b, HALO + at)[1]
            to_l, to_r = x, x
            if g is not None:
                to_l = jnp.where(lane < 12, x, turn(g, 12))
                to_r = jnp.where(lane < 116, turn(g, -12), x)
            slot = (lane >= 16 * s) & (lane < 16 * s + 16)
            left = jnp.where(slot, turn(to_l, 16 * s), left)
            right = jnp.where(slot, turn(to_r, 16 * s - 112), right)
        to_a[k] = jnp.where(col_even, right, left)
        to_b[k] = jnp.where(col_even, left, right)


def weights_kernel(taps, out):
    for m, (layer, flip) in enumerate(((0, False), (1, False), (1, True), (0, True))):
        tiles = [taps[9 * layer + n] for n in range(9)]
        if flip:
            tiles = [tile.T for tile in tiles]
        hi, lo = split(jnp.concatenate(tiles, axis=1))
        out[m, :C] = hi
        out[m, C:] = lo


def dot(a, b):
    return jnp.dot(a, b, preferred_element_type=F32)


def split(value):
    hi = value.astype(BF16)
    lo = (value - hi.astype(F32)).astype(BF16)
    return hi, lo


def weighted(weights, x_hi, x_lo):
    both = dot(weights, x_hi)
    low = dot(weights[:C], x_lo)
    return both[:C] + (both[C:] + low)


def main_kernel(
    dil, pair, cot, row_a, row_b, col_a, col_b, fields, wts, pair_out, send,
    x0, xh, xl, yh, yl, sh, sl, gm, sides, merged, t0s, s0s, g1s, buf,
):
    d0, d1 = dil[0], dil[1]
    row, col = lax.axis_index("row"), lax.axis_index("col")
    lane = lanes_of(C)
    row_even, col_even = row % 2 == 0, col % 2 == 0
    own_u = spread(fields[2 * col], fields[2 * col + 1])
    side_u = spread(fields[jnp.minimum(2 * col + 2, PEERS - 1)], fields[jnp.maximum(2 * col - 1, 0)])
    group, core = row // 2, row % 2
    near = jnp.clip(group - 1 + core, 0, PEERS - 1)
    far = jnp.clip(group + core, 0, PEERS - 1)
    row_u = turn(spread(fields[near], fields[far]), 76 + 32 * core)
    inside = ((lane < HALO) & (col < 7)) | ((lane >= COLS - HALO) & (col > 0))
    side_mask = jnp.where(inside, 1.0, 0.0).astype(F32)
    side_u = side_u * side_mask

    def row_mask(e):
        at = row * ROWS + e - HALO
        return jnp.where((at >= 0) & (at < BINS), 1.0, 0.0).astype(F32)

    def put_shifted(hi_ref, lo_ref, e, main, side, step, swap):
        low = lane < step
        high = lane >= COLS - step
        for ref, a, b in zip((hi_ref, lo_ref), split(main), split(side)):
            up = turn(jnp.where(high, b, a), step)
            down = turn(jnp.where(low, b, a), COLS - step)
            if swap:
                ref[e, :C] = down
                ref[e, C : 2 * C] = a
                ref[e, 2 * C :] = up
            else:
                ref[e, :C, :COLS] = up
                ref[e, :C, COLS:] = turn(jnp.where(high, a, b), step)
                ref[e, C : 2 * C, :COLS] = a
                ref[e, C : 2 * C, COLS:] = b
                ref[e, 2 * C :, :COLS] = down
                ref[e, 2 * C :, COLS:] = turn(jnp.where(low, a, b), COLS - step)

    lower = lane % 32 < 16
    for k in range(EXT // 8):
        fl, fr = partners(col_even, col_a, col_b, k)
        merged[0, k] = jnp.where(lower, fl, turn(fr, 16))
        merged[1, k] = jnp.where(lower, turn(fl, -16), fr)
    near_sides = (lane < HALO) | (lane >= COLS - HALO)
    one_hot = jnp.where(
        lax.broadcasted_iota(jnp.int32, (COLS, 8 * COLS), 0)
        == lax.broadcasted_iota(jnp.int32, (COLS, 8 * COLS), 1) // COLS, 1.0, 0.0,
    ).astype(BF16)

    def fanned(values):
        both = dot(jnp.concatenate(split(values), axis=0), one_hot)
        return both[:C] + both[C:]

    def assemble(e, k, s, x, ui, keep):
        side = turn(merged[s % 2, k], -16 * s if s % 2 else -16 * s - 16)
        sides[e] = side
        side = jnp.where(near_sides, side, 0.0)
        u_main, u_side = ui + own_u, ui * side_mask + side_u
        if keep is not None:
            u_main, u_side = u_main * keep, u_side * keep
        main = x + u_main
        side = side + u_side
        x0[e, :, :COLS] = main
        x0[e, :, COLS:] = side
        put_shifted(xh, xl, e, main, side, d0, False)

    fan_low = fanned(row_u), fanned(turn(row_u, -8))
    fan_high = fanned(turn(row_u, -(HALO + ROWS))), fanned(turn(row_u, -(HALO + ROWS + 8)))
    for at in range(HALO):
        above, below = partners(row_even, row_a, row_b, at)
        e, f = at, at + HALO + ROWS
        part = slice((at % 8) * COLS, (at % 8 + 1) * COLS)
        assemble(e, e // 8, e % 8, above, fan_low[at // 8][:, part], row_mask(e))
        assemble(f, f // 8, f % 8, below, fan_high[at // 8][:, part], row_mask(f))

    def assemble_own(q, carry):
        fan = fanned(turn(row_u, (COLS - HALO - 8 * q) % COLS))
        for s in range(8):
            k, slot = q + 1 + (s + 4) // 8, (s + 4) % 8
            at = 8 * q + s
            assemble(
                at + HALO, k, slot, pair[pl.ds(at, C, stride=ROWS), :], fan[:, s * COLS : (s + 1) * COLS], None
            )
        return carry

    lax.fori_loop(0, ROWS // 8, assemble_own, 0)

    def stacked(ref, lowest, middle, highest):
        return jnp.concatenate([ref[lowest], ref[middle], ref[highest]], axis=0)

    def first(i, carry):
        e = i + 4
        acc = weighted(
            wts[0], stacked(xh, e - d0, e, e + d0), stacked(xl, e - d0, e, e + d0)
        )
        t = jnp.tanh(acc)
        t0s[e] = t[:, :COLS]
        keep = row_mask(e)
        main = x0[e, :, :COLS] + t[:, :COLS] * keep
        side = x0[e, :, COLS:] + t[:, COLS:] * (side_mask * keep)
        x0[e, :, :COLS] = main
        put_shifted(yh, yl, e, main, side, d1, False)
        return carry

    lax.fori_loop(0, EXT - 8, first, 0, unroll=16)

    def second(e, own):
        acc = weighted(
            wts[1], stacked(yh, e - d1, e, e + d1), stacked(yl, e - d1, e, e + d1)
        )
        t = jnp.tanh(acc)
        if own:
            pair_out[pl.ds(e - HALO, C, stride=ROWS), :] = x0[e, :, :COLS] + t[:, :COLS]
        slope = 1.0 - t * t
        if own:
            g = cot[pl.ds(e - HALO, C, stride=ROWS), :]
            gm[e - HALO] = g
        elif e < HALO:
            g = partners(row_even, row_a, row_b, HALO + e - 8)[0]
        else:
            g = partners(row_even, row_a, row_b, e - ROWS)[1]
        side = sides[e]
        g_side = jnp.where(
            lane < GHALO, turn(side, -12), jnp.where(lane >= COLS - GHALO, turn(side, 12), 0.0)
        )
        put_shifted(sh, sl, e - 8, g * slope[:, :COLS], g_side * slope[:, COLS:], d1, True)

    def second_own(i, carry):
        second(i + HALO, True)
        return carry

    for e in (8, 9, 10, 11, 44, 45, 46, 47):
        second(e, False)
    lax.fori_loop(0, ROWS, second_own, 0, unroll=16)

    def third(i, carry):
        parts_hi, parts_lo = [], []
        for k in range(2):
            q = 2 * i + k + GHALO
            parts_hi.append(stacked(sh, q + d1, q, q - d1))
            parts_lo.append(stacked(sl, q + d1, q, q - d1))
        acc = weighted(
            wts[2], jnp.concatenate(parts_hi, axis=1), jnp.concatenate(parts_lo, axis=1)
        )
        for k in range(2):
            at = 2 * i + k
            g1 = gm[at] + acc[:, k * COLS : (k + 1) * COLS]
            t = t0s[at + HALO]
            g1s[at] = g1
            s0s[at] = g1 * (1.0 - t * t)
        return carry

    lax.fori_loop(0, ROWS // 2, third, 0, unroll=8)

    lane8 = lanes_of(8)
    edge = ((lane8 < d0) & (col == 0)) | ((lane8 >= COLS - d0) & (col == 7))
    edge_lanes = jnp.where(edge, 1.0, 0.0).astype(F32)
    first_col = jnp.where(col == 0, 1.0, 0.0).astype(F32)
    last_col = jnp.where(col == 7, 1.0, 0.0).astype(F32)
    pieces = []
    for octet in range(C // 8):
        at = slice(8 * octet, 8 * octet + 8)
        cg = c0 = rg = r0 = re = top = bottom = jnp.zeros((8, COLS), F32)
        for i in range(ROWS):
            s0, g1 = s0s[i, at], g1s[i, at]
            cg, c0 = cg + g1, c0 + s0
            here = lane8 == i
            rg = jnp.where(here, jnp.sum(g1, axis=1, keepdims=True), rg)
            r0 = jnp.where(here, jnp.sum(s0, axis=1, keepdims=True), r0)
            re = jnp.where(here, jnp.sum(s0 * edge_lanes, axis=1, keepdims=True), re)
            if i < GHALO:
                top = top + s0 * jnp.where((row == 0) & (i < d0), 1.0, 0.0).astype(F32)
            if i >= ROWS - GHALO:
                bottom = bottom + s0 * jnp.where((row == 31) & (i >= ROWS - d0), 1.0, 0.0).astype(F32)
        pieces.append((cg, c0 - top, c0, c0 - bottom, rg, r0 - re * first_col, r0, r0 - re * last_col))
    cg, cd, c0, cu, rg, rd, r0, ru = [jnp.concatenate(p, axis=0) for p in zip(*pieces)]
    zero = jnp.zeros((C, COLS), F32)
    blocks = []
    for part in (cd, c0, cu):
        wide = jnp.concatenate([part, zero], axis=1)
        blocks += [turn(wide, 256 - d0), wide, turn(wide, d0)]
    col_x = jnp.concatenate(blocks, axis=0)
    blocks = []
    for a in range(3):
        for part in (rd, r0, ru):
            blocks.append((turn(part, COLS - d0), part, turn(part, d0))[a])
    row_x = jnp.concatenate(blocks, axis=0)
    hi, lo = split(jnp.concatenate([col_x, row_x], axis=1))
    made = weighted(wts[3], hi, lo)
    buf[...] = jnp.zeros(buf.shape, F32)

    def add(first_at, second_at, value):
        one, two = packed(value)
        buf[first_at] = buf[first_at] + one
        buf[second_at] = buf[second_at] + two

    add(2 * col + 1, 2 * col + 2, cg + made[:, :COLS])
    add(2 * col + 3, 2 * col, made[:, COLS : 2 * COLS])
    add(group + core, group + core + 1, turn(rg + made[:, 2 * COLS :], 64 - 32 * core))
    send[...] = buf[1 : PEERS + 1]


def layers(dilation, pair, cot, row_a, row_b, col_a, col_b, fields, wts):
    return pl.pallas_call(
        main_kernel,
        in_specs=[SMEM] + [VMEM] * 8,
        out_specs=[VMEM] * 2,
        out_shape=[
            jax.ShapeDtypeStruct((C * ROWS, COLS), F32),
            jax.ShapeDtypeStruct((PEERS, C // 2, COLS), F32),
        ],
        scratch_shapes=[
            pltpu.VMEM((EXT, C, 2 * COLS), F32),
            pltpu.VMEM((EXT, 3 * C, 2 * COLS), BF16),
            pltpu.VMEM((EXT, 3 * C, 2 * COLS), BF16),
            pltpu.VMEM((EXT, 3 * C, 2 * COLS), BF16),
            pltpu.VMEM((EXT, 3 * C, 2 * COLS), BF16),
            pltpu.VMEM((GEXT, 3 * C, COLS), BF16),
            pltpu.VMEM((GEXT, 3 * C, COLS), BF16),
            pltpu.VMEM((ROWS, C, COLS), F32),
            pltpu.VMEM((EXT, C, COLS), F32),
            pltpu.VMEM((2, EXT // 8, C, COLS), F32),
            pltpu.VMEM((EXT, C, COLS), F32),
            pltpu.VMEM((ROWS, C, COLS), F32),
            pltpu.VMEM((ROWS, C, COLS), F32),
            pltpu.VMEM((PEERS + 2, C // 2, COLS), F32),
        ],
        compiler_params=pltpu.CompilerParams(vmem_limit_bytes=40 * 2**20),
        name="layers",
    )(dilation, pair, cot, row_a, row_b, col_a, col_b, fields, wts)


def finish_kernel(parts, proj_t, out):
    core = lax.axis_index("row") % 2
    total = parts[0]
    for peer in range(1, PEERS):
        total = total + parts[peer]
    both = jnp.concatenate([turn(total, 128 - 32 * core), turn(total, 64 - 32 * core)], axis=0)
    grad = lax.dot_general(
        both, proj_t[...], (((0,), (0,)), ((), ())),
        precision=lax.Precision.HIGHEST, preferred_element_type=F32,
    )
    out[...] = grad[:ROWS]


def local(embed, proj, pair_in, kernels, dilation, cotangent):
    rows, cols = 32, 8
    row_first = [(i, i ^ 1) for i in range(rows)]
    row_second = [(i, ((i + 1) ^ 1) - 1) for i in range(1, rows - 1)]
    col_first = [(i, i ^ 1) for i in range(cols)]
    col_second = [(i, ((i + 1) ^ 1) - 1) for i in range(1, cols - 1)]
    same_core = [[2 * i + core for i in range(PEERS)] for core in range(2)]
    chips = [[(2 * g + core) * cols + c for core in range(2) for c in range(cols)] for g in range(PEERS)]
    packs = jax.ShapeDtypeStruct((PEERS, C // 2, COLS), F32)
    proj_t = proj.T

    pair = pair_in.reshape(C * ROWS, COLS)
    cot = cotangent.reshape(C * ROWS, COLS)
    edge_a, edge_b = pl.pallas_call(
        edges_kernel, in_specs=[VMEM] * 2, out_specs=[VMEM] * 2,
        out_shape=[jax.ShapeDtypeStruct((HALO + GHALO, C, COLS), F32)] * 2, name="edges",
        compiler_params=pltpu.CompilerParams(vmem_limit_bytes=8 * 2**20),
    )(pair, cot)
    edge_a, edge_b, embed = lax.optimization_barrier((edge_a, edge_b, embed))
    row_b = lax.ppermute(edge_b, "row", row_second)
    row_a = lax.ppermute(edge_a, "row", row_first)

    parts = pl.pallas_call(
        project_kernel, in_specs=[VMEM, VMEM], out_specs=VMEM, out_shape=packs, name="project",
    )(embed, proj_t)
    parts = lax.all_to_all(parts, ("row", "col"), 0, 0, tiled=True, axis_index_groups=chips)

    strip_a, strip_b = pl.pallas_call(
        strips_kernel,
        in_specs=[VMEM] * 4,
        out_specs=[VMEM] * 2,
        out_shape=[jax.ShapeDtypeStruct((EXT // 8, C, COLS), F32)] * 2,
        compiler_params=pltpu.CompilerParams(vmem_limit_bytes=8 * 2**20),
        name="strips",
    )(pair, cot, row_a, row_b)
    parts, strip_a, strip_b = lax.optimization_barrier((parts, strip_a, strip_b))
    col_b = lax.ppermute(strip_b, "col", col_second)
    col_a = lax.ppermute(strip_a, "col", col_first)

    own = jnp.sum(parts, axis=0)
    fields = jnp.broadcast_to(own, (PEERS,) + own.shape)
    fields = lax.all_to_all(fields, "row", 0, 0, tiled=True, axis_index_groups=same_core)

    taps = kernels.transpose(0, 3, 4, 1, 2).reshape(18, C, C)
    wts = pl.pallas_call(
        weights_kernel, in_specs=[VMEM], out_specs=VMEM,
        out_shape=jax.ShapeDtypeStruct((4, 2 * C, TAPS), BF16), name="weights",
    )(taps)
    pair_out, send = layers(dilation, pair, cot, row_a, row_b, col_a, col_b, fields, wts)

    got = lax.all_to_all(send, "row", 0, 0, tiled=True, axis_index_groups=same_core)
    own = jnp.sum(got, axis=0)
    got = lax.all_to_all(
        jnp.broadcast_to(own, (PEERS,) + own.shape), ("row", "col"), 0, 0, tiled=True, axis_index_groups=chips
    )
    embed_grad = pl.pallas_call(
        finish_kernel, in_specs=[VMEM, VMEM], out_specs=VMEM,
        out_shape=jax.ShapeDtypeStruct((ROWS, 64), F32), name="finish",
    )(got, proj_t)
    return (pair_out.reshape(C, ROWS, COLS), embed_grad)


def solution(mesh):
    in_specs = (
        P("row", "col"),
        P("col", None),
        P(None, "row", "col"),
        P(),
        P(),
        P(None, "row", "col"),
    )
    out_specs = (P(None, "row", "col"), P("row", "col"))
    return jax.shard_map(local, mesh=mesh, in_specs=in_specs, out_specs=out_specs, check_vma=False)
```

```python
import functools

import jax
import jax.numpy as jnp
from jax import lax
from jax.experimental import pallas as pl
from jax.experimental.pallas import tpu as pltpu
from jax.sharding import PartitionSpec as P

C = 48
ROWS = 32
COLS = 128
HALO = 12
GHALO = 4
EXT = ROWS + 2 * HALO
GEXT = ROWS + 2 * GHALO
TAPS = 9 * C
BINS = 1024
PEERS = 16
F32 = jnp.float32
BF16 = jnp.bfloat16
VMEM = pl.BlockSpec(memory_space=pltpu.VMEM)
SMEM = pl.BlockSpec(memory_space=pltpu.SMEM)
SMALL = pltpu.CompilerParams(vmem_limit_bytes=4 * 2**20)


def lanes_of(rows, width=COLS):
    return lax.broadcasted_iota(jnp.int32, (rows, width), 1)


def turn(value, shift):
    width = value.shape[-1]
    if isinstance(shift, int):
        shift = shift % width
        if shift == 0:
            return value
    return pltpu.roll(value, shift, value.ndim - 1)


def spread(first, second):
    low = lanes_of(C // 2) < 64
    top = jnp.where(low, first, turn(second, 64))
    bottom = jnp.where(low, turn(first, 64), second)
    return jnp.concatenate([top, bottom], axis=0)


def packed(value):
    low = lanes_of(C // 2) < 64
    top, bottom = value[: C // 2], value[C // 2 :]
    first = jnp.where(low, top, turn(bottom, 64))
    second = jnp.where(low, turn(top, 64), bottom)
    return first, second


def open_kernel(embed_hbm, proj_hbm, pair_hbm, cot_hbm, out, to_a, to_b, embed, proj_t, pair, cot, sems):
    copies = [
        pltpu.make_async_copy(source_, target, sems.at[n])
        for n, (source_, target) in enumerate(
            ((embed_hbm, embed), (proj_hbm, proj_t), (pair_hbm, pair), (cot_hbm, cot))
        )
    ]
    for copy in copies:
        copy.start()
    row = lax.axis_index("row")
    core = row % 2
    copies[0].wait()
    copies[1].wait()
    part = lax.dot_general(
        proj_t[...], embed[...], (((1,), (1,)), ((), ())),
        precision=lax.Precision.HIGHEST, preferred_element_type=F32,
    )
    part = jnp.concatenate([part, jnp.zeros((C, COLS - ROWS), F32)], axis=1)
    mine = turn(part[: C // 2], 32 * core) + turn(part[C // 2 :], 64 + 32 * core)
    for peer in range(PEERS):
        out[peer] = mine
    even = core == 0
    for copy, ref, count, start in ((copies[2], pair, HALO, 0), (copies[3], cot, GHALO, HALO)):
        copy.wait()
        for e in range(count):
            low = ref[pl.ds(e + ROWS - count, C, stride=ROWS), :]
            high = ref[pl.ds(e, C, stride=ROWS), :]
            to_a[start + e] = jnp.where(even, low, high)
            to_b[start + e] = jnp.where(even, high, low)


def partners(mine_is_even, got_a, got_b, at):
    one, two = got_a[at], got_b[at]
    return jnp.where(mine_is_even, two, one), jnp.where(mine_is_even, one, two)


def source(e):
    if e < HALO:
        return 0, e
    if e < HALO + ROWS:
        return 1, e - HALO
    return 2, e - HALO - ROWS


def edges_kernel(pair, cot, to_a, to_b):
    even = lax.axis_index("row") % 2 == 0
    for ref, count, start in ((pair, HALO, 0), (cot, GHALO, HALO)):
        for e in range(count):
            low = ref[pl.ds(e + ROWS - count, C, stride=ROWS), :]
            high = ref[pl.ds(e, C, stride=ROWS), :]
            to_a[start + e] = jnp.where(even, low, high)
            to_b[start + e] = jnp.where(even, high, low)


def strips_kernel(pair, cot, got_a, got_b, to_a, to_b):
    lane = lanes_of(C)
    row_even = lax.axis_index("row") % 2 == 0
    col_even = lax.axis_index("col") % 2 == 0
    for k in range(EXT // 8):
        left = jnp.zeros((C, COLS), F32)
        right = jnp.zeros((C, COLS), F32)
        for s in range(8):
            e = 8 * k + s
            place, at = source(e)
            g = None
            if place == 1:
                x = pair[pl.ds(at, C, stride=ROWS), :]
                g = cot[pl.ds(at, C, stride=ROWS), :]
            elif place == 0:
                x = partners(row_even, got_a, got_b, at)[0]
                if e >= 8:
                    g = partners(row_even, got_a, got_b, HALO + e - 8)[0]
            else:
                x = partners(row_even, got_a, got_b, at)[1]
                if at < GHALO:
                    g = partners(row_even, got_a, got_b, HALO + at)[1]
            to_l, to_r = x, x
            if g is not None:
                to_l = jnp.where(lane < 12, x, turn(g, 12))
                to_r = jnp.where(lane < 116, turn(g, -12), x)
            slot = (lane >= 16 * s) & (lane < 16 * s + 16)
            left = jnp.where(slot, turn(to_l, 16 * s), left)
            right = jnp.where(slot, turn(to_r, 16 * s - 112), right)
        to_a[k] = jnp.where(col_even, right, left)
        to_b[k] = jnp.where(col_even, left, right)


def weights_kernel(taps, out):
    for m, (layer, flip) in enumerate(((0, False), (1, False), (1, True), (0, True))):
        tiles = [taps[9 * layer + n] for n in range(9)]
        if flip:
            tiles = [tile.T for tile in tiles]
        hi, lo = split(jnp.concatenate(tiles, axis=1))
        out[m, :C] = hi
        out[m, C:] = lo


def dot(a, b):
    return jnp.dot(a, b, preferred_element_type=F32)


def split(value):
    hi = value.astype(BF16)
    lo = (value - hi.astype(F32)).astype(BF16)
    return hi, lo


def weighted(weights, x_hi, x_lo):
    both = dot(weights, x_hi)
    low = dot(weights[:C], x_lo)
    return both[:C] + (both[C:] + low)


def main_kernel(
    dil, pair, cot, row_a, row_b, col_a, col_b, fields, wts, pair_out, send,
    x0, xh, xl, yh, yl, sh, sl, gm, sides, merged, t0s, s0s, g1s, buf, kept, sem,
):
    d0, d1 = dil[0], dil[1]
    row, col = lax.axis_index("row"), lax.axis_index("col")
    lane = lanes_of(C)
    row_even, col_even = row % 2 == 0, col % 2 == 0
    own_u = spread(fields[2 * col], fields[2 * col + 1])
    side_u = spread(fields[jnp.minimum(2 * col + 2, PEERS - 1)], fields[jnp.maximum(2 * col - 1, 0)])
    group, core = row // 2, row % 2
    near = jnp.clip(group - 1 + core, 0, PEERS - 1)
    far = jnp.clip(group + core, 0, PEERS - 1)
    row_u = turn(spread(fields[near], fields[far]), 76 + 32 * core)
    inside = ((lane < HALO) & (col < 7)) | ((lane >= COLS - HALO) & (col > 0))
    side_mask = jnp.where(inside, 1.0, 0.0).astype(F32)
    side_u = side_u * side_mask

    def row_mask(e):
        at = row * ROWS + e - HALO
        return jnp.where((at >= 0) & (at < BINS), 1.0, 0.0).astype(F32)

    def put_shifted(hi_ref, lo_ref, e, main, side, step, swap):
        low = lane < step
        high = lane >= COLS - step
        for ref, a, b in zip((hi_ref, lo_ref), split(main), split(side)):
            up = turn(jnp.where(high, b, a), step)
            down = turn(jnp.where(low, b, a), COLS - step)
            if swap:
                ref[e, :C] = down
                ref[e, C : 2 * C] = a
                ref[e, 2 * C :] = up
            else:
                ref[e, :C, :COLS] = up
                ref[e, :C, COLS:] = turn(jnp.where(high, a, b), step)
                ref[e, C : 2 * C, :COLS] = a
                ref[e, C : 2 * C, COLS:] = b
                ref[e, 2 * C :, :COLS] = down
                ref[e, 2 * C :, COLS:] = turn(jnp.where(low, a, b), COLS - step)

    lower = lane % 32 < 16
    for k in range(EXT // 8):
        fl, fr = partners(col_even, col_a, col_b, k)
        merged[0, k] = jnp.where(lower, fl, turn(fr, 16))
        merged[1, k] = jnp.where(lower, turn(fl, -16), fr)
    near_sides = (lane < HALO) | (lane >= COLS - HALO)
    one_hot = jnp.where(
        lax.broadcasted_iota(jnp.int32, (COLS, 8 * COLS), 0)
        == lax.broadcasted_iota(jnp.int32, (COLS, 8 * COLS), 1) // COLS, 1.0, 0.0,
    ).astype(BF16)

    def fanned(values):
        both = dot(jnp.concatenate(split(values), axis=0), one_hot)
        return both[:C] + both[C:]

    def assemble(e, k, s, x, ui, keep):
        side = turn(merged[s % 2, k], -16 * s if s % 2 else -16 * s - 16)
        sides[e] = side
        side = jnp.where(near_sides, side, 0.0)
        u_main, u_side = ui + own_u, ui * side_mask + side_u
        if keep is not None:
            u_main, u_side = u_main * keep, u_side * keep
        main = x + u_main
        side = side + u_side
        x0[e, :, :COLS] = main
        x0[e, :, COLS:] = side
        put_shifted(xh, xl, e, main, side, d0, False)

    fan_low = fanned(row_u), fanned(turn(row_u, -8))
    fan_high = fanned(turn(row_u, -(HALO + ROWS))), fanned(turn(row_u, -(HALO + ROWS + 8)))
    for at in range(HALO):
        above, below = partners(row_even, row_a, row_b, at)
        e, f = at, at + HALO + ROWS
        part = slice((at % 8) * COLS, (at % 8 + 1) * COLS)
        assemble(e, e // 8, e % 8, above, fan_low[at // 8][:, part], row_mask(e))
        assemble(f, f // 8, f % 8, below, fan_high[at // 8][:, part], row_mask(f))

    def assemble_own(q, carry):
        fan = fanned(turn(row_u, (COLS - HALO - 8 * q) % COLS))
        for s in range(8):
            k, slot = q + 1 + (s + 4) // 8, (s + 4) % 8
            at = 8 * q + s
            assemble(
                at + HALO, k, slot, pair[pl.ds(at, C, stride=ROWS), :], fan[:, s * COLS : (s + 1) * COLS], None
            )
        return carry

    lax.fori_loop(0, ROWS // 8, assemble_own, 0)

    def stacked(ref, lowest, middle, highest):
        return jnp.concatenate([ref[lowest], ref[middle], ref[highest]], axis=0)

    def first(i, carry):
        e = i + 4
        acc = weighted(
            wts[0], stacked(xh, e - d0, e, e + d0), stacked(xl, e - d0, e, e + d0)
        )
        t = jnp.tanh(acc)
        t0s[e] = t[:, :COLS]
        keep = row_mask(e)
        main = x0[e, :, :COLS] + t[:, :COLS] * keep
        side = x0[e, :, COLS:] + t[:, COLS:] * (side_mask * keep)
        x0[e, :, :COLS] = main
        put_shifted(yh, yl, e, main, side, d1, False)
        return carry

    lax.fori_loop(0, EXT - 8, first, 0, unroll=48)

    def second(e, own):
        acc = weighted(
            wts[1], stacked(yh, e - d1, e, e + d1), stacked(yl, e - d1, e, e + d1)
        )
        t = jnp.tanh(acc)
        if own:
            kept[pl.ds(e - HALO, C, stride=ROWS), :] = x0[e, :, :COLS] + t[:, :COLS]
        slope = 1.0 - t * t
        if own:
            g = cot[pl.ds(e - HALO, C, stride=ROWS), :]
            gm[e - HALO] = g
        elif e < HALO:
            g = partners(row_even, row_a, row_b, HALO + e - 8)[0]
        else:
            g = partners(row_even, row_a, row_b, e - ROWS)[1]
        side = sides[e]
        g_side = jnp.where(
            lane < GHALO, turn(side, -12), jnp.where(lane >= COLS - GHALO, turn(side, 12), 0.0)
        )
        put_shifted(sh, sl, e - 8, g * slope[:, :COLS], g_side * slope[:, COLS:], d1, True)

    def second_own(i, carry):
        second(i + HALO, True)
        return carry

    for e in (8, 9, 10, 11, 44, 45, 46, 47):
        second(e, False)
    lax.fori_loop(0, ROWS, second_own, 0, unroll=32)

    copy = pltpu.make_async_copy(kept, pair_out, sem)
    copy.start()

    def third(i, carry):
        parts_hi, parts_lo = [], []
        for k in range(2):
            q = 2 * i + k + GHALO
            parts_hi.append(stacked(sh, q + d1, q, q - d1))
            parts_lo.append(stacked(sl, q + d1, q, q - d1))
        acc = weighted(
            wts[2], jnp.concatenate(parts_hi, axis=1), jnp.concatenate(parts_lo, axis=1)
        )
        for k in range(2):
            at = 2 * i + k
            g1 = gm[at] + acc[:, k * COLS : (k + 1) * COLS]
            t = t0s[at + HALO]
            g1s[at] = g1
            s0s[at] = g1 * (1.0 - t * t)
        return carry

    lax.fori_loop(0, ROWS // 2, third, 0, unroll=16)

    lane8 = lanes_of(8)
    edge = ((lane8 < d0) & (col == 0)) | ((lane8 >= COLS - d0) & (col == 7))
    edge_lanes = jnp.where(edge, 1.0, 0.0).astype(F32)
    first_col = jnp.where(col == 0, 1.0, 0.0).astype(F32)
    last_col = jnp.where(col == 7, 1.0, 0.0).astype(F32)
    pieces = []
    for octet in range(C // 8):
        at = slice(8 * octet, 8 * octet + 8)
        cg = c0 = rg = r0 = re = top = bottom = jnp.zeros((8, COLS), F32)
        for i in range(ROWS):
            s0, g1 = s0s[i, at], g1s[i, at]
            cg, c0 = cg + g1, c0 + s0
            here = lane8 == i
            rg = jnp.where(here, jnp.sum(g1, axis=1, keepdims=True), rg)
            r0 = jnp.where(here, jnp.sum(s0, axis=1, keepdims=True), r0)
            re = jnp.where(here, jnp.sum(s0 * edge_lanes, axis=1, keepdims=True), re)
            if i < GHALO:
                top = top + s0 * jnp.where((row == 0) & (i < d0), 1.0, 0.0).astype(F32)
            if i >= ROWS - GHALO:
                bottom = bottom + s0 * jnp.where((row == 31) & (i >= ROWS - d0), 1.0, 0.0).astype(F32)
        pieces.append((cg, c0 - top, c0, c0 - bottom, rg, r0 - re * first_col, r0, r0 - re * last_col))
    cg, cd, c0, cu, rg, rd, r0, ru = [jnp.concatenate(p, axis=0) for p in zip(*pieces)]
    zero = jnp.zeros((C, COLS), F32)
    blocks = []
    for part in (cd, c0, cu):
        wide = jnp.concatenate([part, zero], axis=1)
        blocks += [turn(wide, 256 - d0), wide, turn(wide, d0)]
    col_x = jnp.concatenate(blocks, axis=0)
    blocks = []
    for a in range(3):
        for part in (rd, r0, ru):
            blocks.append((turn(part, COLS - d0), part, turn(part, d0))[a])
    row_x = jnp.concatenate(blocks, axis=0)
    hi, lo = split(jnp.concatenate([col_x, row_x], axis=1))
    made = weighted(wts[3], hi, lo)
    buf[...] = jnp.zeros(buf.shape, F32)

    def add(first_at, second_at, value):
        one, two = packed(value)
        buf[first_at] = buf[first_at] + one
        buf[second_at] = buf[second_at] + two

    add(2 * col + 1, 2 * col + 2, cg + made[:, :COLS])
    add(2 * col + 3, 2 * col, made[:, COLS : 2 * COLS])
    add(group + core, group + core + 1, turn(rg + made[:, 2 * COLS :], 64 - 32 * core))
    send[...] = buf[1 : PEERS + 1]
    copy.wait()


def layers(dilation, pair, cot, row_a, row_b, col_a, col_b, fields, wts):
    return pl.pallas_call(
        main_kernel,
        in_specs=[SMEM] + [VMEM] * 8,
        out_specs=[pl.BlockSpec(memory_space=pl.ANY), VMEM],
        out_shape=[
            jax.ShapeDtypeStruct((C * ROWS, COLS), F32),
            jax.ShapeDtypeStruct((PEERS, C // 2, COLS), F32),
        ],
        scratch_shapes=[
            pltpu.VMEM((EXT, C, 2 * COLS), F32),
            pltpu.VMEM((EXT, 3 * C, 2 * COLS), BF16),
            pltpu.VMEM((EXT, 3 * C, 2 * COLS), BF16),
            pltpu.VMEM((EXT, 3 * C, 2 * COLS), BF16),
            pltpu.VMEM((EXT, 3 * C, 2 * COLS), BF16),
            pltpu.VMEM((GEXT, 3 * C, COLS), BF16),
            pltpu.VMEM((GEXT, 3 * C, COLS), BF16),
            pltpu.VMEM((ROWS, C, COLS), F32),
            pltpu.VMEM((EXT, C, COLS), F32),
            pltpu.VMEM((2, EXT // 8, C, COLS), F32),
            pltpu.VMEM((EXT, C, COLS), F32),
            pltpu.VMEM((ROWS, C, COLS), F32),
            pltpu.VMEM((ROWS, C, COLS), F32),
            pltpu.VMEM((PEERS + 2, C // 2, COLS), F32),
            pltpu.VMEM((C * ROWS, COLS), F32),
            pltpu.SemaphoreType.DMA,
        ],
        compiler_params=pltpu.CompilerParams(vmem_limit_bytes=36 * 2**20),
        name="layers",
    )(dilation, pair, cot, row_a, row_b, col_a, col_b, fields, wts)


def finish_kernel(parts, proj_t, out):
    core = lax.axis_index("row") % 2
    total = parts[0]
    for peer in range(1, PEERS):
        total = total + parts[peer]
    both = jnp.concatenate([turn(total, 128 - 32 * core), turn(total, 64 - 32 * core)], axis=0)
    grad = lax.dot_general(
        both, proj_t[...], (((0,), (0,)), ((), ())),
        precision=lax.Precision.HIGHEST, preferred_element_type=F32,
    )
    out[...] = grad[:ROWS]


def local(embed, proj, pair_in, kernels, dilation, cotangent):
    rows, cols = 32, 8
    row_first = [(i, i ^ 1) for i in range(rows)]
    row_second = [(i, ((i + 1) ^ 1) - 1) for i in range(1, rows - 1)]
    col_first = [(i, i ^ 1) for i in range(cols)]
    col_second = [(i, ((i + 1) ^ 1) - 1) for i in range(1, cols - 1)]
    same_core = [[2 * i + core for i in range(PEERS)] for core in range(2)]
    chips = [[(2 * g + core) * cols + c for core in range(2) for c in range(cols)] for g in range(PEERS)]
    packs = jax.ShapeDtypeStruct((PEERS, C // 2, COLS), F32)
    proj_t = proj.T

    pair = pair_in.reshape(C * ROWS, COLS)
    cot = cotangent.reshape(C * ROWS, COLS)
    any_space = pl.BlockSpec(memory_space=pltpu.HBM)
    edge = jax.ShapeDtypeStruct((HALO + GHALO, C, COLS), F32)
    parts, edge_a, edge_b = pl.pallas_call(
        open_kernel, in_specs=[any_space] * 4, out_specs=[VMEM] * 3, out_shape=[packs, edge, edge],
        scratch_shapes=[
            pltpu.VMEM((ROWS, 64), F32),
            pltpu.VMEM((C, 64), F32),
            pltpu.VMEM((C * ROWS, COLS), F32),
            pltpu.VMEM((C * ROWS, COLS), F32),
            pltpu.SemaphoreType.DMA((4,)),
        ],
        compiler_params=pltpu.CompilerParams(vmem_limit_bytes=60 * 2**20), name="open",
    )(embed, proj_t, pair, cot)
    row_b = lax.ppermute(edge_b, "row", row_second)
    row_a = lax.ppermute(edge_a, "row", row_first)

    parts = lax.all_to_all(parts, ("row", "col"), 0, 0, tiled=True, axis_index_groups=chips)

    strip_a, strip_b = pl.pallas_call(
        strips_kernel,
        in_specs=[VMEM] * 4,
        out_specs=[VMEM] * 2,
        out_shape=[jax.ShapeDtypeStruct((EXT // 8, C, COLS), F32)] * 2,
        compiler_params=SMALL,
        name="strips",
    )(pair, cot, row_a, row_b)
    taps = kernels.transpose(0, 3, 4, 1, 2).reshape(18, C, C)
    wts = pl.pallas_call(
        weights_kernel, in_specs=[VMEM], out_specs=VMEM,
        out_shape=jax.ShapeDtypeStruct((4, 2 * C, TAPS), BF16), name="weights",
        compiler_params=SMALL,
    )(taps)
    parts, strip_a, strip_b, wts = lax.optimization_barrier((parts, strip_a, strip_b, wts))
    col_b = lax.ppermute(strip_b, "col", col_second)
    col_a = lax.ppermute(strip_a, "col", col_first)

    own = jnp.sum(parts, axis=0)
    fields = jnp.broadcast_to(own, (PEERS,) + own.shape)
    fields = lax.all_to_all(fields, "row", 0, 0, tiled=True, axis_index_groups=same_core)

    pair_out, send = layers(dilation, pair, cot, row_a, row_b, col_a, col_b, fields, wts)

    got = lax.all_to_all(send, "row", 0, 0, tiled=True, axis_index_groups=same_core)
    own = jnp.sum(got, axis=0)
    got = lax.all_to_all(
        jnp.broadcast_to(own, (PEERS,) + own.shape), ("row", "col"), 0, 0, tiled=True, axis_index_groups=chips
    )
    embed_grad = pl.pallas_call(
        finish_kernel, in_specs=[VMEM, VMEM], out_specs=VMEM,
        out_shape=jax.ShapeDtypeStruct((ROWS, 64), F32), name="finish",
        compiler_params=SMALL,
    )(got, proj_t)
    return (pair_out.reshape(C, ROWS, COLS), embed_grad)


def solution(mesh):
    in_specs = (
        P("row", "col"),
        P("col", None),
        P(None, "row", "col"),
        P(),
        P(),
        P(None, "row", "col"),
    )
    out_specs = (P(None, "row", "col"), P("row", "col"))
    return jax.shard_map(local, mesh=mesh, in_specs=in_specs, out_specs=out_specs, check_vma=False)
```

```python
import functools

import jax
import jax.numpy as jnp
from jax import lax
from jax.experimental import pallas as pl
from jax.experimental.pallas import tpu as pltpu
from jax.sharding import PartitionSpec as P

C = 48
ROWS = 32
COLS = 128
HALO = 12
GHALO = 4
EXT = ROWS + 2 * HALO
GEXT = ROWS + 2 * GHALO
TAPS = 9 * C
BINS = 1024
PEERS = 16
F32 = jnp.float32
BF16 = jnp.bfloat16
VMEM = pl.BlockSpec(memory_space=pltpu.VMEM)
SMEM = pl.BlockSpec(memory_space=pltpu.SMEM)
SMALL = pltpu.CompilerParams(vmem_limit_bytes=4 * 2**20)


def lanes_of(rows, width=COLS):
    return lax.broadcasted_iota(jnp.int32, (rows, width), 1)


def turn(value, shift):
    width = value.shape[-1]
    if isinstance(shift, int):
        shift = shift % width
        if shift == 0:
            return value
    return pltpu.roll(value, shift, value.ndim - 1)


def spread(first, second):
    low = lanes_of(C // 2) < 64
    top = jnp.where(low, first, turn(second, 64))
    bottom = jnp.where(low, turn(first, 64), second)
    return jnp.concatenate([top, bottom], axis=0)


def packed(value):
    low = lanes_of(C // 2) < 64
    top, bottom = value[: C // 2], value[C // 2 :]
    first = jnp.where(low, top, turn(bottom, 64))
    second = jnp.where(low, turn(top, 64), bottom)
    return first, second


def open_kernel(embed_hbm, proj_hbm, pair_hbm, cot_hbm, out, to_a, to_b, embed, proj_t, pair, cot, sems):
    copies = [
        pltpu.make_async_copy(source_, target, sems.at[n])
        for n, (source_, target) in enumerate(
            ((embed_hbm, embed), (proj_hbm, proj_t), (pair_hbm, pair), (cot_hbm, cot))
        )
    ]
    for copy in copies:
        copy.start()
    row = lax.axis_index("row")
    core = row % 2
    copies[0].wait()
    copies[1].wait()
    part = lax.dot_general(
        proj_t[...], embed[...], (((1,), (1,)), ((), ())),
        precision=lax.Precision.HIGHEST, preferred_element_type=F32,
    )
    part = jnp.concatenate([part, jnp.zeros((C, COLS - ROWS), F32)], axis=1)
    mine = turn(part[: C // 2], 32 * core) + turn(part[C // 2 :], 64 + 32 * core)
    for peer in range(PEERS):
        out[peer] = mine
    even = core == 0
    for copy, ref, count, start in ((copies[2], pair, HALO, 0), (copies[3], cot, GHALO, HALO)):
        copy.wait()
        for e in range(count):
            low = ref[pl.ds(e + ROWS - count, C, stride=ROWS), :]
            high = ref[pl.ds(e, C, stride=ROWS), :]
            to_a[start + e] = jnp.where(even, low, high)
            to_b[start + e] = jnp.where(even, high, low)


def partners(mine_is_even, got_a, got_b, at):
    one, two = got_a[at], got_b[at]
    return jnp.where(mine_is_even, two, one), jnp.where(mine_is_even, one, two)


def source(e):
    if e < HALO:
        return 0, e
    if e < HALO + ROWS:
        return 1, e - HALO
    return 2, e - HALO - ROWS


def edges_kernel(pair, cot, to_a, to_b):
    even = lax.axis_index("row") % 2 == 0
    for ref, count, start in ((pair, HALO, 0), (cot, GHALO, HALO)):
        for e in range(count):
            low = ref[pl.ds(e + ROWS - count, C, stride=ROWS), :]
            high = ref[pl.ds(e, C, stride=ROWS), :]
            to_a[start + e] = jnp.where(even, low, high)
            to_b[start + e] = jnp.where(even, high, low)


def combine_kernel(parts, out):
    total = parts[0]
    for peer in range(1, PEERS):
        total = total + parts[peer]
    for peer in range(PEERS):
        out[peer] = total


def strips_kernel(pair, cot, got_a, got_b, to_a, to_b):
    lane = lanes_of(C)
    row_even = lax.axis_index("row") % 2 == 0
    col_even = lax.axis_index("col") % 2 == 0
    for k in range(EXT // 8):
        left = jnp.zeros((C, COLS), F32)
        right = jnp.zeros((C, COLS), F32)
        for s in range(8):
            e = 8 * k + s
            place, at = source(e)
            g = None
            if place == 1:
                x = pair[pl.ds(at, C, stride=ROWS), :]
                g = cot[pl.ds(at, C, stride=ROWS), :]
            elif place == 0:
                x = partners(row_even, got_a, got_b, at)[0]
                if e >= 8:
                    g = partners(row_even, got_a, got_b, HALO + e - 8)[0]
            else:
                x = partners(row_even, got_a, got_b, at)[1]
                if at < GHALO:
                    g = partners(row_even, got_a, got_b, HALO + at)[1]
            to_l, to_r = x, x
            if g is not None:
                to_l = jnp.where(lane < 12, x, turn(g, 12))
                to_r = jnp.where(lane < 116, turn(g, -12), x)
            slot = (lane >= 16 * s) & (lane < 16 * s + 16)
            left = jnp.where(slot, turn(to_l, 16 * s), left)
            right = jnp.where(slot, turn(to_r, 16 * s - 112), right)
        to_a[k] = jnp.where(col_even, right, left)
        to_b[k] = jnp.where(col_even, left, right)


def weights_kernel(taps, out):
    for m, (layer, flip) in enumerate(((0, False), (1, False), (1, True), (0, True))):
        tiles = [taps[9 * layer + n] for n in range(9)]
        if flip:
            tiles = [tile.T for tile in tiles]
        hi, lo = split(jnp.concatenate(tiles, axis=1))
        out[m, :C] = hi
        out[m, C:] = lo


def dot(a, b):
    return jnp.dot(a, b, preferred_element_type=F32)


def split(value):
    hi = value.astype(BF16)
    lo = (value - hi.astype(F32)).astype(BF16)
    return hi, lo


def weighted(weights, x_hi, x_lo):
    both = dot(weights, x_hi)
    low = dot(weights[:C], x_lo)
    return both[:C] + (both[C:] + low)


def main_kernel(
    dil, pair, cot, row_a, row_b, col_a, col_b, fields, wts, pair_out, send,
    x0, mh, ml, xh, xl, yh, yl, sh, sl, gm, sides, merged, t0s, s0s, g1s, buf, kept, sem,
):
    d0, d1 = dil[0], dil[1]
    row, col = lax.axis_index("row"), lax.axis_index("col")
    lane = lanes_of(C)
    row_even, col_even = row % 2 == 0, col % 2 == 0
    own_u = spread(fields[2 * col], fields[2 * col + 1])
    side_u = spread(fields[jnp.minimum(2 * col + 2, PEERS - 1)], fields[jnp.maximum(2 * col - 1, 0)])
    group, core = row // 2, row % 2
    near = jnp.clip(group - 1 + core, 0, PEERS - 1)
    far = jnp.clip(group + core, 0, PEERS - 1)
    row_u = turn(spread(fields[near], fields[far]), 76 + 32 * core)
    inside = ((lane < HALO) & (col < 7)) | ((lane >= COLS - HALO) & (col > 0))
    side_mask = jnp.where(inside, 1.0, 0.0).astype(F32)
    side_u = side_u * side_mask

    def row_mask(e):
        at = row * ROWS + e - HALO
        return jnp.where((at >= 0) & (at < BINS), 1.0, 0.0).astype(F32)

    def put_shifted(hi_ref, lo_ref, e, main, side, step, swap):
        low = lane < step
        high = lane >= COLS - step
        for ref, a, b in zip((hi_ref, lo_ref), split(main), split(side)):
            up = turn(jnp.where(high, b, a), step)
            down = turn(jnp.where(low, b, a), COLS - step)
            if swap:
                ref[e, :C] = down
                ref[e, C : 2 * C] = a
                ref[e, 2 * C :] = up
            else:
                ref[e, :C, :COLS] = up
                ref[e, :C, COLS:] = turn(jnp.where(high, a, b), step)
                ref[e, C : 2 * C, :COLS] = a
                ref[e, C : 2 * C, COLS:] = b
                ref[e, 2 * C :, :COLS] = down
                ref[e, 2 * C :, COLS:] = turn(jnp.where(low, a, b), COLS - step)

    lower = lane % 32 < 16
    for k in range(EXT // 8):
        fl, fr = partners(col_even, col_a, col_b, k)
        merged[0, k] = jnp.where(lower, fl, turn(fr, 16))
        merged[1, k] = jnp.where(lower, turn(fl, -16), fr)
    near_sides = (lane < HALO) | (lane >= COLS - HALO)
    one_hot = jnp.where(
        lax.broadcasted_iota(jnp.int32, (COLS, 8 * COLS), 0)
        == lax.broadcasted_iota(jnp.int32, (COLS, 8 * COLS), 1) // COLS, 1.0, 0.0,
    ).astype(BF16)

    source_lane = lax.broadcasted_iota(jnp.int32, (2 * COLS, 4 * COLS), 0)
    target_lane = lax.broadcasted_iota(jnp.int32, (2 * COLS, 4 * COLS), 1)
    wanted = jnp.where(target_lane < 2 * COLS, target_lane - d0, target_lane + d0) & (2 * COLS - 1)
    shifts = jnp.where(source_lane == wanted, 1.0, 0.0).astype(BF16)

    def shift_rows(e, count):
        rows = pl.ds(e, count)
        for middle, ref in ((mh, xh), (ml, xl)):
            moved = dot(middle[rows].reshape(count * C, 2 * COLS), shifts)
            moved = moved.astype(BF16).reshape(count, C, 4 * COLS)
            ref[rows, :C] = moved[:, :, : 2 * COLS]
            ref[rows, C:] = moved[:, :, 2 * COLS :]

    def fanned(values):
        both = dot(jnp.concatenate(split(values), axis=0), one_hot)
        return both[:C] + both[C:]

    def assemble(e, k, s, x, ui, keep):
        side = turn(merged[s % 2, k], -16 * s if s % 2 else -16 * s - 16)
        sides[e] = side
        side = jnp.where(near_sides, side, 0.0)
        u_main, u_side = ui + own_u, ui * side_mask + side_u
        if keep is not None:
            u_main, u_side = u_main * keep, u_side * keep
        main = x + u_main
        side = side + u_side
        x0[e, :, :COLS] = main
        x0[e, :, COLS:] = side
        for ref, a, b in zip((mh, ml), split(main), split(side)):
            ref[e, :, :COLS] = a
            ref[e, :, COLS:] = b

    fan_low = fanned(row_u), fanned(turn(row_u, -8))
    fan_high = fanned(turn(row_u, -(HALO + ROWS))), fanned(turn(row_u, -(HALO + ROWS + 8)))
    for at in range(HALO):
        above, below = partners(row_even, row_a, row_b, at)
        e, f = at, at + HALO + ROWS
        part = slice((at % 8) * COLS, (at % 8 + 1) * COLS)
        assemble(e, e // 8, e % 8, above, fan_low[at // 8][:, part], row_mask(e))
        assemble(f, f // 8, f % 8, below, fan_high[at // 8][:, part], row_mask(f))

    def assemble_own(q, carry):
        shift_rows(8 * q + 4, 8)
        fan = fanned(turn(row_u, (COLS - HALO - 8 * q) % COLS))
        for s in range(8):
            k, slot = q + 1 + (s + 4) // 8, (s + 4) % 8
            at = 8 * q + s
            assemble(
                at + HALO, k, slot, pair[pl.ds(at, C, stride=ROWS), :], fan[:, s * COLS : (s + 1) * COLS], None
            )
        return carry

    lax.fori_loop(0, ROWS // 8, assemble_own, 0)
    shift_rows(0, 4)
    shift_rows(HALO + ROWS - 8, HALO + 8)

    def stacked(ref, lowest, middle, highest):
        return jnp.concatenate([ref[lowest], ref[middle], ref[highest]], axis=0)

    def first(i, carry):
        e = i + 4
        x_hi, x_lo = (
            jnp.concatenate(
                [piece for at in (e - d0, e, e + d0) for piece in (ref[at, :C], middle[at], ref[at, C:])], axis=0
            )
            for ref, middle in ((xh, mh), (xl, ml))
        )
        acc = weighted(wts[0], x_hi, x_lo)
        t = jnp.tanh(acc)
        t0s[e] = t[:, :COLS]
        keep = row_mask(e)
        main = x0[e, :, :COLS] + t[:, :COLS] * keep
        side = x0[e, :, COLS:] + t[:, COLS:] * (side_mask * keep)
        x0[e, :, :COLS] = main
        put_shifted(yh, yl, e, main, side, d1, False)
        return carry

    lax.fori_loop(0, EXT - 8, first, 0, unroll=48)

    def second(e, own):
        acc = weighted(
            wts[1], stacked(yh, e - d1, e, e + d1), stacked(yl, e - d1, e, e + d1)
        )
        t = jnp.tanh(acc)
        if own:
            kept[pl.ds(e - HALO, C, stride=ROWS), :] = x0[e, :, :COLS] + t[:, :COLS]
        slope = 1.0 - t * t
        if own:
            g = cot[pl.ds(e - HALO, C, stride=ROWS), :]
            gm[e - HALO] = g
        elif e < HALO:
            g = partners(row_even, row_a, row_b, HALO + e - 8)[0]
        else:
            g = partners(row_even, row_a, row_b, e - ROWS)[1]
        side = sides[e]
        g_side = jnp.where(
            lane < GHALO, turn(side, -12), jnp.where(lane >= COLS - GHALO, turn(side, 12), 0.0)
        )
        put_shifted(sh, sl, e - 8, g * slope[:, :COLS], g_side * slope[:, COLS:], d1, True)

    def second_own(i, carry):
        second(i + HALO, True)
        return carry

    for e in (8, 9, 10, 11, 44, 45, 46, 47):
        second(e, False)
    lax.fori_loop(0, ROWS, second_own, 0, unroll=32)

    copy = pltpu.make_async_copy(kept, pair_out, sem)
    copy.start()

    def third(i, carry):
        parts_hi, parts_lo = [], []
        for k in range(2):
            q = 2 * i + k + GHALO
            parts_hi.append(stacked(sh, q + d1, q, q - d1))
            parts_lo.append(stacked(sl, q + d1, q, q - d1))
        acc = weighted(
            wts[2], jnp.concatenate(parts_hi, axis=1), jnp.concatenate(parts_lo, axis=1)
        )
        for k in range(2):
            at = 2 * i + k
            g1 = gm[at] + acc[:, k * COLS : (k + 1) * COLS]
            t = t0s[at + HALO]
            g1s[at] = g1
            s0s[at] = g1 * (1.0 - t * t)
        return carry

    lax.fori_loop(0, ROWS // 2, third, 0, unroll=16)

    lane8 = lanes_of(8)
    edge = ((lane8 < d0) & (col == 0)) | ((lane8 >= COLS - d0) & (col == 7))
    edge_lanes = jnp.where(edge, 1.0, 0.0).astype(F32)
    first_col = jnp.where(col == 0, 1.0, 0.0).astype(F32)
    last_col = jnp.where(col == 7, 1.0, 0.0).astype(F32)
    pieces = []
    for octet in range(C // 8):
        at = slice(8 * octet, 8 * octet + 8)
        cg = c0 = rg = r0 = re = top = bottom = jnp.zeros((8, COLS), F32)
        for i in range(ROWS):
            s0, g1 = s0s[i, at], g1s[i, at]
            cg, c0 = cg + g1, c0 + s0
            here = lane8 == i
            rg = jnp.where(here, jnp.sum(g1, axis=1, keepdims=True), rg)
            r0 = jnp.where(here, jnp.sum(s0, axis=1, keepdims=True), r0)
            re = jnp.where(here, jnp.sum(s0 * edge_lanes, axis=1, keepdims=True), re)
            if i < GHALO:
                top = top + s0 * jnp.where((row == 0) & (i < d0), 1.0, 0.0).astype(F32)
            if i >= ROWS - GHALO:
                bottom = bottom + s0 * jnp.where((row == 31) & (i >= ROWS - d0), 1.0, 0.0).astype(F32)
        pieces.append((cg, c0 - top, c0, c0 - bottom, rg, r0 - re * first_col, r0, r0 - re * last_col))
    cg, cd, c0, cu, rg, rd, r0, ru = [jnp.concatenate(p, axis=0) for p in zip(*pieces)]
    zero = jnp.zeros((C, COLS), F32)
    blocks = []
    for part in (cd, c0, cu):
        wide = jnp.concatenate([part, zero], axis=1)
        blocks += [turn(wide, 256 - d0), wide, turn(wide, d0)]
    col_x = jnp.concatenate(blocks, axis=0)
    blocks = []
    for a in range(3):
        for part in (rd, r0, ru):
            blocks.append((turn(part, COLS - d0), part, turn(part, d0))[a])
    row_x = jnp.concatenate(blocks, axis=0)
    hi, lo = split(jnp.concatenate([col_x, row_x], axis=1))
    made = weighted(wts[3], hi, lo)
    buf[...] = jnp.zeros(buf.shape, F32)

    def add(first_at, second_at, value):
        one, two = packed(value)
        buf[first_at] = buf[first_at] + one
        buf[second_at] = buf[second_at] + two

    add(2 * col + 1, 2 * col + 2, cg + made[:, :COLS])
    add(2 * col + 3, 2 * col, made[:, COLS : 2 * COLS])
    add(group + core, group + core + 1, turn(rg + made[:, 2 * COLS :], 64 - 32 * core))
    send[...] = buf[1 : PEERS + 1]
    copy.wait()


def layers(dilation, pair, cot, row_a, row_b, col_a, col_b, fields, wts):
    return pl.pallas_call(
        main_kernel,
        in_specs=[SMEM] + [VMEM] * 8,
        out_specs=[pl.BlockSpec(memory_space=pl.ANY), VMEM],
        out_shape=[
            jax.ShapeDtypeStruct((C * ROWS, COLS), F32),
            jax.ShapeDtypeStruct((PEERS, C // 2, COLS), F32),
        ],
        scratch_shapes=[
            pltpu.VMEM((EXT, C, 2 * COLS), F32),
            pltpu.VMEM((EXT, C, 2 * COLS), BF16),
            pltpu.VMEM((EXT, C, 2 * COLS), BF16),
            pltpu.VMEM((EXT, 2 * C, 2 * COLS), BF16),
            pltpu.VMEM((EXT, 2 * C, 2 * COLS), BF16),
            pltpu.VMEM((EXT, 3 * C, 2 * COLS), BF16),
            pltpu.VMEM((EXT, 3 * C, 2 * COLS), BF16),
            pltpu.VMEM((GEXT, 3 * C, COLS), BF16),
            pltpu.VMEM((GEXT, 3 * C, COLS), BF16),
            pltpu.VMEM((ROWS, C, COLS), F32),
            pltpu.VMEM((EXT, C, COLS), F32),
            pltpu.VMEM((2, EXT // 8, C, COLS), F32),
            pltpu.VMEM((EXT, C, COLS), F32),
            pltpu.VMEM((ROWS, C, COLS), F32),
            pltpu.VMEM((ROWS, C, COLS), F32),
            pltpu.VMEM((PEERS + 2, C // 2, COLS), F32),
            pltpu.VMEM((C * ROWS, COLS), F32),
            pltpu.SemaphoreType.DMA,
        ],
        compiler_params=pltpu.CompilerParams(vmem_limit_bytes=36 * 2**20),
        name="layers",
    )(dilation, pair, cot, row_a, row_b, col_a, col_b, fields, wts)


def finish_kernel(parts, proj_t, out):
    core = lax.axis_index("row") % 2
    total = parts[0]
    for peer in range(1, PEERS):
        total = total + parts[peer]
    both = jnp.concatenate([turn(total, 128 - 32 * core), turn(total, 64 - 32 * core)], axis=0)
    grad = lax.dot_general(
        both, proj_t[...], (((0,), (0,)), ((), ())),
        precision=lax.Precision.HIGHEST, preferred_element_type=F32,
    )
    out[...] = grad[:ROWS]


def local(embed, proj, pair_in, kernels, dilation, cotangent):
    rows, cols = 32, 8
    row_first = [(i, i ^ 1) for i in range(rows)]
    row_second = [(i, ((i + 1) ^ 1) - 1) for i in range(1, rows - 1)]
    col_first = [(i, i ^ 1) for i in range(cols)]
    col_second = [(i, ((i + 1) ^ 1) - 1) for i in range(1, cols - 1)]
    same_core = [[2 * i + core for i in range(PEERS)] for core in range(2)]
    chips = [[(2 * g + core) * cols + c for core in range(2) for c in range(cols)] for g in range(PEERS)]
    packs = jax.ShapeDtypeStruct((PEERS, C // 2, COLS), F32)
    proj_t = proj.T

    pair = pair_in.reshape(C * ROWS, COLS)
    cot = cotangent.reshape(C * ROWS, COLS)
    any_space = pl.BlockSpec(memory_space=pltpu.HBM)
    edge = jax.ShapeDtypeStruct((HALO + GHALO, C, COLS), F32)
    parts, edge_a, edge_b = pl.pallas_call(
        open_kernel, in_specs=[any_space] * 4, out_specs=[VMEM] * 3, out_shape=[packs, edge, edge],
        scratch_shapes=[
            pltpu.VMEM((ROWS, 64), F32),
            pltpu.VMEM((C, 64), F32),
            pltpu.VMEM((C * ROWS, COLS), F32),
            pltpu.VMEM((C * ROWS, COLS), F32),
            pltpu.SemaphoreType.DMA((4,)),
        ],
        compiler_params=pltpu.CompilerParams(vmem_limit_bytes=60 * 2**20), name="open",
    )(embed, proj_t, pair, cot)
    row_b = lax.ppermute(edge_b, "row", row_second)
    row_a = lax.ppermute(edge_a, "row", row_first)

    parts = lax.all_to_all(parts, ("row", "col"), 0, 0, tiled=True, axis_index_groups=chips)

    strip_a, strip_b = pl.pallas_call(
        strips_kernel,
        in_specs=[VMEM] * 4,
        out_specs=[VMEM] * 2,
        out_shape=[jax.ShapeDtypeStruct((EXT // 8, C, COLS), F32)] * 2,
        compiler_params=SMALL,
        name="strips",
    )(pair, cot, row_a, row_b)
    taps = kernels.transpose(0, 3, 4, 1, 2).reshape(18, C, C)
    wts = pl.pallas_call(
        weights_kernel, in_specs=[VMEM], out_specs=VMEM,
        out_shape=jax.ShapeDtypeStruct((4, 2 * C, TAPS), BF16), name="weights",
        compiler_params=SMALL,
    )(taps)
    parts, strip_a, strip_b, wts = lax.optimization_barrier((parts, strip_a, strip_b, wts))
    col_b = lax.ppermute(strip_b, "col", col_second)
    col_a = lax.ppermute(strip_a, "col", col_first)

    fields = pl.pallas_call(
        combine_kernel, in_specs=[VMEM], out_specs=VMEM, out_shape=packs,
        compiler_params=pltpu.CompilerParams(vmem_limit_bytes=2 * 2**20), name="combine",
    )(parts)
    fields = lax.all_to_all(fields, "row", 0, 0, tiled=True, axis_index_groups=same_core)

    pair_out, send = layers(dilation, pair, cot, row_a, row_b, col_a, col_b, fields, wts)

    got = lax.all_to_all(send, "row", 0, 0, tiled=True, axis_index_groups=same_core)
    own = jnp.sum(got, axis=0)
    got = lax.all_to_all(
        jnp.broadcast_to(own, (PEERS,) + own.shape), ("row", "col"), 0, 0, tiled=True, axis_index_groups=chips
    )
    embed_grad = pl.pallas_call(
        finish_kernel, in_specs=[VMEM, VMEM], out_specs=VMEM,
        out_shape=jax.ShapeDtypeStruct((ROWS, 64), F32), name="finish",
        compiler_params=SMALL,
    )(got, proj_t)
    return (pair_out.reshape(C, ROWS, COLS), embed_grad)


def solution(mesh):
    in_specs = (
        P("row", "col"),
        P("col", None),
        P(None, "row", "col"),
        P(),
        P(),
        P(None, "row", "col"),
    )
    out_specs = (P(None, "row", "col"), P("row", "col"))
    return jax.shard_map(local, mesh=mesh, in_specs=in_specs, out_specs=out_specs, check_vma=False)
```
